256 devices in a mesh: section: 16 (over z, y_hi), dp: 16 (over y_lo, x, core).
Axes of the slice: x: 4, y: 4 (y_hi: 2, y_lo: 2; y = y_hi * 2 + y_lo), z: 8, core: 2. Of those that a mesh axis runs over, the one named last changes fastest.
Arguments:
- tokens: bfloat16 [8, 256, 8192], P(None, 'dp'), may hold values from -6 to 6
- cotangent: bfloat16 [8, 256, 8192], P(None, 'dp'), may hold values from -0.119628906 to 0.119628906
- sample_ids: int32 [16, 8], P('dp'), may hold values from 0 to 7, each once within a row
- sent_before: bfloat16 [16, 128, 16, 8192], P('section', 'dp'), may hold values from -1.796875 to 1.796875
- received_before: bfloat16 [16, 128, 16, 8192], P('section', 'dp'), may hold values from -1.796875 to 1.796875
- norm_gain: float32 [16, 8192], P('section'), may hold values from 0.5 to 2
- down_proj: bfloat16 [16, 8192, 256], P('section', 'dp'), may hold values from -0.0625 to 0.0625
- up_proj: bfloat16 [16, 256, 8192], P('section', None, 'dp'), may hold values from -0.375 to 0.375
Outputs:
- grad_down: float32 [16, 8192, 256], P('section', 'dp')
- grad_up: float32 [16, 256, 8192], P('section', None, 'dp')
The draws below stay inside these ranges and needn't reach their ends.
Inputs may be any that keep to these rules, and one draw needn't show every extreme that they name: Each row of sample_ids, one replica's micro-batches, names each of its 8 stored samples once.
All inputs are finite; a program needn't handle non-finite values.
Results may differ from the reference program's by a relative error of at most 0.035.
Values may be sent and summed in bfloat16 or wider, within the bound.
A program may use at most 128 MiB of HBM per device.

```python
import math
import jax
import jax.numpy as jnp
from jax import lax

D = 8192
RANK = 256
TOK = 16
MICRO = 8
TOKENS = 256
SLOTS = 128
N_SECTION = 16
N_DP = 16


def spiked(array, stream_key, source, target, shards_of, factor):
    def block_of(position):
        return (jnp.arange(array.shape[position]) // (array.shape[position] // shards_of)).reshape((-1,) + (1,) * (array.ndim - 1 - position))

    one_side = jax.random.permutation(stream_key, shards_of)[block_of(target)]
    other_side = (block_of(target) + shards_of // 2) % shards_of
    return jnp.where((block_of(source) == one_side) | (block_of(source) == other_side), factor * array, array)


def levels(rng, extent, split, least, largest):
    def one(dim, parts):
        steps = jax.random.uniform(jax.random.fold_in(jax.random.fold_in(rng, 6), dim), (parts,), jnp.float32, least / len(split), largest / len(split))
        return jnp.repeat(jnp.exp(steps), extent[dim] // parts).reshape((-1,) + (1,) * (len(extent) - dim - 1))

    loudness = one(*split[0])
    for cut in split[1:]:
        loudness = loudness * one(*cut)
    return loudness


def noise(stream_key, dims, width, reach, split=(), kind=jnp.bfloat16):
    array = jax.random.normal(stream_key, dims, jnp.float32) * width
    if len(split) > 0:
        array = levels(stream_key, dims, split, -0.22, 0.18) * array
    return jnp.clip(array, min=-reach, max=reach).astype(kind)


def noise_with(own_key, shape, width, limit, split, heavy, held_as=jnp.bfloat16):
    entries = width * jax.random.normal(own_key, shape, jnp.float32)
    if split:
        entries = entries * levels(own_key, shape, split, -0.22, 0.18)
    return jnp.clip(spiked(entries, jax.random.fold_in(own_key, 3), *heavy), -limit, limit).astype(held_as)


def setup_inputs(seed: int = 0) -> dict:
    key_list = jax.random.split(jax.random.key(seed), 9)
    tokens = noise(key_list[0], (MICRO, TOKENS, D), 1.0, 6.0, ((1, 16),))
    cotangent = noise_with(key_list[1], (MICRO, TOKENS, D), 0.02, 0.119628906, ((1, 16),), (1, 2, 16, 2.0))
    sample_ids = jax.vmap(lambda own: jax.random.permutation(own, MICRO))(jax.random.split(key_list[2], N_DP)).reshape((N_DP, MICRO)).astype(jnp.int32)
    sent_before = noise(key_list[3], (N_SECTION, SLOTS, TOK, D), 0.3, 1.796875, ((0, 16), (1, 16)))
    received_before = noise(key_list[4], (N_SECTION, SLOTS, TOK, D), 0.3, 1.796875, ((0, 16), (1, 16)))
    norm_gain = jnp.clip(jnp.exp(math.log(2.0) - 1.3862944 * jax.random.uniform(key_list[5], (N_SECTION, D), jnp.float32) ** levels(key_list[5], (N_SECTION, D), ((0, 16),), -0.2, 0.2)), 0.5, 2.0)
    down_proj = noise(key_list[6], (N_SECTION, D, RANK), D ** -0.5, 0.0625, ((0, 16), (1, 16)))
    up_proj = noise(key_list[7], (N_SECTION, RANK, D), RANK ** -0.5, 0.375, ((0, 16), (2, 16)))
    return dict(tokens=tokens, cotangent=cotangent, sample_ids=sample_ids, sent_before=sent_before, received_before=received_before, norm_gain=norm_gain, down_proj=down_proj, up_proj=up_proj)


epsilon = 1e-05

def normalize(activation, gain_row, down_weight):
    row_scale = lax.rsqrt(lax.optimization_barrier(jnp.mean(activation * activation, axis=-1, keepdims=True)) + epsilon)
    normed = (activation * row_scale * gain_row).astype(jnp.bfloat16)
    pre_act = jnp.dot(normed, down_weight, preferred_element_type=jnp.float32)
    active = jax.nn.silu(pre_act).astype(jnp.bfloat16)
    return (row_scale, normed, pre_act, active)

def transposed(operand_a, operand_b):
    return lax.dot_general(operand_a, operand_b, (((1,), (1,)), ((), ())), preferred_element_type=jnp.float32)

def backward_layer(activation, upstream, gain_row, down_weight, up_weight):
    row_scale, normed, pre_act, active = normalize(activation, gain_row, down_weight)
    upstream_b = upstream.astype(jnp.bfloat16)
    d_active = transposed(upstream_b, up_weight)
    gate_sig = jax.nn.sigmoid(pre_act)
    d_pre = (d_active * gate_sig * (1.0 + pre_act * (1.0 - gate_sig))).astype(jnp.bfloat16)
    d_normed = transposed(d_pre, down_weight) * gain_row
    d_state = upstream + row_scale * d_normed - activation * row_scale ** 3 * lax.optimization_barrier(jnp.mean(d_normed * activation, axis=-1, keepdims=True))
    return (d_state, normed, active, upstream_b, d_pre)

def pick_rows(table, sample_ids, micro_now):
    offsets = jnp.arange(N_DP, dtype=jnp.int32) * MICRO
    chosen = table[offsets + sample_ids[:, micro_now].astype(jnp.int32)]
    return chosen.reshape(N_DP * TOK, D)

def per_replica(left_rows, right_rows):
    left_part = left_rows.astype(jnp.float32).reshape(MICRO, N_DP, TOK, -1)
    right_part = right_rows.astype(jnp.float32).reshape(MICRO, N_DP, TOK, -1)
    partial_sums = jnp.einsum('mrta,mrtb->rab', left_part, right_part)
    rounded = lax.optimization_barrier(partial_sums.astype(jnp.bfloat16))
    return lax.optimization_barrier(jnp.sum(rounded.astype(jnp.float32), axis=0))

def reference(tokens, cotangent, sample_ids, sent_before, received_before, norm_gain, down_proj, up_proj):
    flat_rows = MICRO * N_DP * TOK
    section_input = tokens.astype(jnp.float32).reshape(flat_rows, D)
    inputs_kept = []
    for section in range(N_SECTION):
        inputs_kept.append(section_input)
        row_scale, normed, pre_act, active = normalize(section_input, norm_gain[section], down_proj[section])
        output = section_input + jnp.dot(active, up_proj[section], preferred_element_type=jnp.float32)
        if section + 1 < N_SECTION:
            previous = jnp.concatenate([pick_rows(sent_before[section], sample_ids, micro_now) for micro_now in range(MICRO)], axis=0)
            change = lax.optimization_barrier((output - previous.astype(jnp.float32)).astype(jnp.bfloat16))
            kept_rows = jnp.concatenate([pick_rows(received_before[section + 1], sample_ids, micro_now) for micro_now in range(MICRO)], axis=0)
            section_input = kept_rows.astype(jnp.float32) + change.astype(jnp.float32)
    upstream = cotangent.astype(jnp.float32).reshape(flat_rows, D)
    grads_down = []
    grads_up = []
    for section in reversed(range(N_SECTION)):
        d_state, normed, active, upstream_b, d_pre = backward_layer(inputs_kept[section], upstream, norm_gain[section], down_proj[section], up_proj[section])
        grads_down.insert(0, per_replica(normed, d_pre))
        grads_up.insert(0, per_replica(active, upstream_b))
        upstream = lax.optimization_barrier(d_state.astype(jnp.bfloat16)).astype(jnp.float32)
    return (jnp.stack(grads_down), jnp.stack(grads_up))
```

```python
import functools

import jax
import jax.numpy as jnp
from jax import lax
from jax.experimental import pallas as pl
from jax.experimental.pallas import tpu as pltpu
from jax.sharding import PartitionSpec as P

MESH = pl.DeviceIdType.MESH
F32, BF16 = jnp.float32, jnp.bfloat16
EPS = 1e-05
D = 8192
HALF = 4096
RANK = 256
TOK = 16
MB = 8
CH = 512
COLS = 1024
NCOL = HALF // COLS
STAGES = 8


def nt(a, b):
    return lax.dot_general(a, b, (((1,), (1,)), ((), ())), preferred_element_type=F32)


def tn(a, b):
    return lax.dot_general(a, b, (((0,), (0,)), ((), ())), preferred_element_type=F32)


def nn(a, b):
    return jnp.dot(a, b, preferred_element_type=F32)


def lanes(v):
    total = v[:, 0:128]
    for k in range(128, v.shape[1], 128):
        total = total + v[:, k : k + 128]
    return total


def kernel(
    rec_in, sent_in, down_in, up_in, gd_out, gu_out,
    rec, sent, wd, wu, xin, uin, xs, um, xf, fout, bout, red_tx, red_rx,
    pre, act, vee, scl, gds, gus, gdl, gul,
    s_tab, r_tab, s_w, r_w, s_hf, r_hf, s_hb, r_hb, s_red, r_red, s_g, r_g,
):
    s = lax.axis_index("section")
    e = lax.axis_index("dp")
    h, z = lax.rem(s, 2), lax.div(s, 2)
    c, q = lax.rem(e, 2), lax.div(e, 2)
    chip = h * 8 + q
    owner_core = lax.div(e, 8)
    local = c == owner_core
    other = (s, e + 1 - 2 * c)

    barrier = pltpu.get_barrier_semaphore()

    def greet(t, carry):
        place = lax.rem(h * 16 + e + t, 32)
        pl.semaphore_signal(
            barrier, inc=1, device_id=(2 * z + lax.div(place, 16), lax.rem(place, 16)), device_id_type=MESH
        )
        return carry

    lax.fori_loop(1, 32, greet, 0)

    @pl.when(z > 0)
    def _():
        pl.semaphore_signal(barrier, inc=1, device_id=(s - 2, e), device_id_type=MESH)

    @pl.when(z < STAGES - 1)
    def _():
        pl.semaphore_signal(barrier, inc=1, device_id=(s + 2, e), device_id_type=MESH)

    neighbours = jnp.where(z > 0, 1, 0) + jnp.where(z < STAGES - 1, 1, 0)
    pl.semaphore_wait(barrier, 31 + neighbours)

    def table_copy(which, k, t):
        src = (rec_in, sent_in)[which]
        dst = (rec, sent)[which]
        h2, c2 = lax.rem(h + t // 2, 2), lax.rem(c + t, 2)
        row = pl.multiple_of((2 * k + c) * TOK, TOK)
        return dict(
            src_ref=src.at[4 * h2 + k, :, pl.ds(pl.multiple_of(c2 * HALF, HALF), HALF)],
            dst_ref=dst.at[h, pl.ds(row, TOK), :],
        ), s_tab.at[which, k, t], r_tab.at[which, h, 2 * k + c], (2 * z + h2, 2 * q + c2)

    def table_start(which, k):
        for t in range(4):
            refs, ssem, rsem, dev = table_copy(which, k, t)
            if t == 0:
                pltpu.make_async_copy(refs["src_ref"], refs["dst_ref"], rsem).start()
            else:
                pltpu.make_async_remote_copy(
                    **refs, send_sem=ssem, recv_sem=rsem, device_id=dev, device_id_type=MESH
                ).start()

    def table_sent(which, k):
        for t in range(1, 4):
            refs, ssem, rsem, dev = table_copy(which, k, t)
            pltpu.make_async_remote_copy(
                **refs, send_sem=ssem, recv_sem=rsem, device_id=dev, device_id_type=MESH
            ).wait_send()

    def table_wait(which, part, i):
        place = (rec, sent)[which].at[part, pl.ds(pl.multiple_of(i * TOK, TOK), TOK), :]
        pltpu.make_async_copy(place, place, r_tab.at[which, part, i]).wait()

    slot = lax.rem(e, 8)
    spot = pl.multiple_of(slot * CH, CH)

    def weight_refs(kind):
        if kind == 0:
            return down_in, wd.at[h, pl.ds(spot, CH), :]
        return up_in, wu.at[h, :, pl.ds(spot, CH)]

    def weight_remote(kind, t):
        src, dst = weight_refs(kind)
        place = lax.rem(chip + t, 16)
        return pltpu.make_async_remote_copy(
            src_ref=src, dst_ref=dst, send_sem=s_w.at[kind, t], recv_sem=r_w.at[kind, h, slot],
            device_id=(2 * z + lax.div(place, 8), 2 * lax.rem(place, 8) + owner_core), device_id_type=MESH,
        )

    def weight_start(kind):
        @pl.when(local)
        def _():
            src, dst = weight_refs(kind)
            pltpu.make_async_copy(src, dst, r_w.at[kind, h, slot]).start()

        @pl.when(jnp.logical_not(local))
        def _():
            weight_remote(kind, 0).start()

        def more(t, carry):
            weight_remote(kind, t).start()
            return carry

        lax.fori_loop(1, 16, more, 0)

    def weight_sent(kind):
        @pl.when(jnp.logical_not(local))
        def _():
            weight_remote(kind, 0).wait_send()

        def more(t, carry):
            weight_remote(kind, t).wait_send()
            return carry

        lax.fori_loop(1, 16, more, 0)

    def weight_wait(kind, part):
        def one(j, carry):
            at = pl.ds(pl.multiple_of(j * CH, CH), CH)
            place = wd.at[part, at, :] if kind == 0 else wu.at[part, :, at]
            pltpu.make_async_copy(place, place, r_w.at[kind, part, j]).wait()
            return carry

        lax.fori_loop(0, 8, one, 0)

    table_start(0, 0)
    weight_start(0)
    weight_start(1)
    table_start(1, 0)
    for k in range(1, 4):
        table_start(0, k)
        table_start(1, k)

    def red_copy(n):
        return pltpu.make_async_remote_copy(
            src_ref=red_tx.at[n], dst_ref=red_rx.at[n], send_sem=s_red.at[n], recv_sem=r_red.at[n],
            device_id=other, device_id_type=MESH,
        )

    def col(n):
        return slice(n * COLS, (n + 1) * COLS)

    def hop(n, i, ahead):
        at = (slice(None), col(n))
        if ahead:
            buf, dst, ss, rs, dev = fout, xin, s_hf, r_hf, (s + 2, e)
        else:
            buf, dst, ss, rs, dev = bout, uin, s_hb, r_hb, (s - 2, e)
        rows = pl.ds(pl.multiple_of(i * TOK, TOK), TOK)
        return pltpu.make_async_remote_copy(
            src_ref=buf.at[rows, col(n)], dst_ref=dst.at[rows, col(n)], send_sem=ss.at[i, n], recv_sem=rs.at[i, n],
            device_id=dev, device_id_type=MESH,
        )

    def forward(i, carry):
        rows = pl.ds(pl.multiple_of(i * TOK, TOK), TOK)
        table_wait(0, 0, i)

        @pl.when(i == 0)
        def _():
            weight_wait(0, 0)

        acc = jnp.zeros((TOK, RANK), F32)
        sq = jnp.zeros((TOK, 128), F32)
        for n in range(NCOL):
            @pl.when(z > 0)
            def _():
                hop(n, i, True).wait_recv()
                xf[:, col(n)] = rec[0, rows, col(n)].astype(F32) + xin[rows, col(n)].astype(F32)

            @pl.when(z == 0)
            def _():
                xf[:, col(n)] = rec[0, rows, col(n)].astype(F32)

            x = xf[:, col(n)]
            xb = x.astype(BF16)
            xs[0, rows, col(n)] = xb
            sq = sq + lanes(x * x)
            acc = acc + nn(xb, wd[0, col(n), :])

        def finish(part, acc, sq):
            n = 2 * i + part
            red_tx[n, :, 0:RANK] = acc
            red_tx[n, :, RANK:] = sq
            red_copy(n).start()
            red_copy(n).wait_recv()
            total = acc + red_rx[n, :, 0:RANK]
            square = jnp.sum(sq + red_rx[n, :, RANK:], axis=1, keepdims=True)
            scale = lax.rsqrt(square * (1.0 / D) + EPS)
            v = total * scale
            pre[part, rows, :] = v
            scl[part, rows, :] = jnp.broadcast_to(scale, (TOK, 128))
            a = (v * jax.nn.sigmoid(v)).astype(BF16)
            act[part, rows, :] = a
            return a

        a = finish(0, acc, sq)

        @pl.when(i == 0)
        def _():
            weight_wait(1, 0)
            weight_wait(0, 1)

        table_wait(0, 1, i)
        table_wait(1, 0, i)
        acc = jnp.zeros((TOK, RANK), F32)
        sq = jnp.zeros((TOK, 128), F32)
        for n in range(NCOL):
            x = (
                xf[:, col(n)] + nn(a, wu[0, :, col(n)])
                + (rec[1, rows, col(n)].astype(F32) - sent[0, rows, col(n)].astype(F32))
            )
            xf[:, col(n)] = x
            xb = x.astype(BF16)
            xs[1, rows, col(n)] = xb
            sq = sq + lanes(x * x)
            acc = acc + nn(xb, wd[1, col(n), :])
        a = finish(1, acc, sq)

        @pl.when(i == 0)
        def _():
            weight_wait(1, 1)

        table_wait(1, 1, i)

        @pl.when(z < STAGES - 1)
        def _():
            for n in range(NCOL):
                x = xf[:, col(n)] + nn(a, wu[1, :, col(n)]) - sent[1, rows, col(n)].astype(F32)
                fout[rows, col(n)] = x.astype(BF16)
                hop(n, i, True).start()

        return carry

    lax.fori_loop(0, MB, forward, 0)

    def backward(i, carry):
        rows = pl.ds(pl.multiple_of(i * TOK, TOK), TOK)
        acc = jnp.zeros((TOK, RANK), F32)
        for n in range(NCOL):
            @pl.when(z < STAGES - 1)
            def _():
                hop(n, i, False).wait_recv()

            @pl.when(z == STAGES - 1)
            def _():
                uin[rows, col(n)] = sent[1, rows, col(n)]

            acc = acc + nt(uin[rows, col(n)], wu[1, :, col(n)])

        def finish(part, acc):
            n = 2 * MB + 2 * i + part
            red_tx[n, :, 0:RANK] = acc
            red_tx[n, :, RANK:] = jnp.zeros((TOK, 128), F32)
            red_copy(n).start()
            red_copy(n).wait_recv()
            total = acc + red_rx[n, :, 0:RANK]
            v = pre[part, rows, :]
            gate = jax.nn.sigmoid(v)
            d_pre = total * gate * (1.0 + v * (1.0 - gate))
            scale = scl[part, rows, 0:1]
            mean = jnp.sum(d_pre * v, axis=1, keepdims=True) * (1.0 / D)
            back = (d_pre * scale).astype(BF16)
            vee[part, rows, :] = back
            return back, mean * scale * scale

        back, shrink = finish(1, acc)
        acc = jnp.zeros((TOK, RANK), F32)
        for n in range(NCOL):
            u = (
                uin[rows, col(n)].astype(F32) + nt(back, wd[1, col(n), :])
                - shrink * xs[1, rows, col(n)].astype(F32)
            ).astype(BF16)
            um[rows, col(n)] = u
            acc = acc + nt(u, wu[0, :, col(n)])
        back, shrink = finish(0, acc)

        @pl.when(z > 0)
        def _():
            for n in range(NCOL):
                u = (
                    um[rows, col(n)].astype(F32) + nt(back, wd[0, col(n), :])
                    - shrink * xs[0, rows, col(n)].astype(F32)
                )
                bout[rows, col(n)] = u.astype(BF16)
                hop(n, i, False).start()

        return carry

    lax.fori_loop(0, MB, backward, 0)

    def grad_copies(t):
        place = lax.rem(chip + t, 16)
        dev = (2 * z + lax.div(place, 8), 8 * c + lax.rem(place, 8))
        return [
            pltpu.make_async_remote_copy(
                src_ref=src.at[t], dst_ref=dst.at[chip], send_sem=s_g.at[kind, t], recv_sem=r_g.at[kind, chip],
                device_id=dev, device_id_type=MESH,
            )
            for kind, src, dst in ((0, gds, gdl), (1, gus, gul))
        ]

    def is_me(t):
        place = lax.rem(chip + t, 16)
        return jnp.logical_and(lax.div(place, 8) == h, 8 * c + lax.rem(place, 8) == e)

    def grads(t, carry):
        place = lax.rem(chip + t, 16)
        part, at = lax.div(place, 8), pl.ds(pl.multiple_of(lax.rem(place, 8) * CH, CH), CH)
        gds[t] = tn(xs[part, :, at], vee[part, :, :]).astype(BF16)

        @pl.when(part == 0)
        def _():
            gus[t] = tn(act[0], um[:, at]).astype(BF16)

        @pl.when(part == 1)
        def _():
            gus[t] = tn(act[1], uin[:, at]).astype(BF16)

        @pl.when(is_me(t))
        def _():
            gdl[chip] = gds[t]
            gul[chip] = gus[t]

        @pl.when(jnp.logical_not(is_me(t)))
        def _():
            for copy in grad_copies(t):
                copy.start()

        return carry

    lax.fori_loop(0, 16, grads, 0)

    gd_out[...] = jnp.zeros_like(gd_out)
    gu_out[...] = jnp.zeros_like(gu_out)

    def gather(t, carry):
        place = lax.rem(chip + 16 - t, 16)

        @pl.when(jnp.logical_not(jnp.logical_and(local, t == 0)))
        def _():
            for kind, dst in ((0, gdl), (1, gul)):
                ref = dst.at[place]
                pltpu.make_async_copy(ref, ref, r_g.at[kind, place]).wait()

        gd_out[...] += gdl[place].astype(F32)
        gu_out[...] += gul[place].astype(F32)
        return carry

    lax.fori_loop(0, 16, gather, 0)

    def grads_sent(t, carry):
        @pl.when(jnp.logical_not(is_me(t)))
        def _():
            for copy in grad_copies(t):
                copy.wait_send()

        return carry

    lax.fori_loop(0, 16, grads_sent, 0)
    weight_sent(0)
    weight_sent(1)
    for k in range(4):
        table_sent(0, k)
        table_sent(1, k)

    def rest(i, carry):
        for n in range(NCOL):
            @pl.when(z < STAGES - 1)
            def _():
                hop(n, i, True).wait_send()

            @pl.when(z > 0)
            def _():
                hop(n, i, False).wait_send()

        for k in range(4):
            red_copy(4 * i + k).wait_send()
        return carry

    lax.fori_loop(0, MB, rest, 0)


def shards(tokens, cotangent, sample_ids, sent_before, received_before, norm_gain, down_proj, up_proj):
    s = lax.axis_index("section")
    e = lax.axis_index("dp")
    last = lax.axis_size("section") - 1
    ids = sample_ids[0]
    micro = jnp.arange(MB, dtype=jnp.int32)
    where_is = jnp.sum(jnp.where(ids[None, :] == micro[:, None], micro[None, :], 0), axis=1)
    rec = jnp.where(s == 0, jnp.take(tokens, where_is, axis=0, mode="clip"), received_before[0])
    sent = jnp.where(s == last, jnp.take(cotangent, where_is, axis=0, mode="clip"), sent_before[0])
    gain = lax.dynamic_slice(norm_gain[0], (e * CH,), (CH,))[:, None]
    down = (down_proj[0].astype(F32) * gain).astype(BF16)
    any_ = pl.BlockSpec(memory_space=pl.ANY)
    vmem = pl.BlockSpec(memory_space=pltpu.VMEM)
    dma = pltpu.SemaphoreType.DMA
    rows = MB * TOK
    grad_down, grad_up = pl.pallas_call(
        kernel,
        out_shape=(jax.ShapeDtypeStruct((CH, RANK), F32), jax.ShapeDtypeStruct((RANK, CH), F32)),
        in_specs=[any_] * 4,
        out_specs=(vmem, vmem),
        scratch_shapes=[
            pltpu.VMEM((2, rows, HALF), BF16),
            pltpu.VMEM((2, rows, HALF), BF16),
            pltpu.VMEM((2, HALF, RANK), BF16),
            pltpu.VMEM((2, RANK, HALF), BF16),
            pltpu.VMEM((rows, HALF), BF16),
            pltpu.VMEM((rows, HALF), BF16),
            pltpu.VMEM((2, rows, HALF), BF16),
            pltpu.VMEM((rows, HALF), BF16),
            pltpu.VMEM((TOK, HALF), F32),
            pltpu.VMEM((rows, HALF), BF16),
            pltpu.VMEM((rows, HALF), BF16),
            pltpu.VMEM((4 * MB, TOK, RANK + 128), F32),
            pltpu.VMEM((4 * MB, TOK, RANK + 128), F32),
            pltpu.VMEM((2, rows, RANK), F32),
            pltpu.VMEM((2, rows, RANK), BF16),
            pltpu.VMEM((2, rows, RANK), BF16),
            pltpu.VMEM((2, rows, 128), F32),
            pltpu.VMEM((16, CH, RANK), BF16),
            pltpu.VMEM((16, RANK, CH), BF16),
            pltpu.VMEM((16, CH, RANK), BF16),
            pltpu.VMEM((16, RANK, CH), BF16),
            dma((2, 4, 4)), dma((2, 2, MB)),
            dma((2, 16)), dma((2, 2, 8)),
            dma((MB, NCOL)), dma((MB, NCOL)),
            dma((MB, NCOL)), dma((MB, NCOL)),
            dma((4 * MB,)), dma((4 * MB,)),
            dma((2, 16)), dma((2, 16)),
        ],
        compiler_params=pltpu.CompilerParams(
            collective_id=0, has_side_effects=True, vmem_limit_bytes=56 * 1024 * 1024
        ),
    )(rec, sent, down, up_proj[0])
    return ((grad_down * gain)[None], grad_up[None])


def solution(mesh):
    placed = (
        P(None, "dp", None),
        P(None, "dp", None),
        P("dp", None),
        P("section", "dp", None, None),
        P("section", "dp", None, None),
        P("section", None),
        P("section", "dp", None),
        P("section", None, "dp"),
    )
    return jax.shard_map(
        shards,
        mesh=mesh,
        in_specs=placed,
        out_specs=(P("section", "dp", None), P("section", None, "dp")),
        check_vma=False,
    )
```

```python
import functools

import jax
import jax.numpy as jnp
from jax import lax
from jax.experimental import pallas as pl
from jax.experimental.pallas import tpu as pltpu
from jax.sharding import PartitionSpec as P

MESH = pl.DeviceIdType.MESH
F32, BF16 = jnp.float32, jnp.bfloat16
EPS = 1e-05
D = 8192
HALF = 4096
RANK = 256
TOK = 16
MB = 8
CH = 512
COLS = 1024
NCOL = HALF // COLS
STAGES = 8
BATCHES = 2
BROWS = MB * TOK // BATCHES


def nt(a, b):
    return lax.dot_general(a, b, (((1,), (1,)), ((), ())), preferred_element_type=F32)


def tn(a, b):
    return lax.dot_general(a, b, (((0,), (0,)), ((), ())), preferred_element_type=F32)


def nn(a, b):
    return jnp.dot(a, b, preferred_element_type=F32)


def lanes(v):
    total = v[:, 0:128]
    for k in range(128, v.shape[1], 128):
        total = total + v[:, k : k + 128]
    return total


def kernel(
    rec_in, sent_in, tok_in, cot_in, down_in, up_in, gd_out, gu_out,
    rec, sent, wd, wu, xin, uin, xs, um, xf, fout, bout, red_tx, red_rx,
    pre, act, vee, scl, gx, ga, gv, gw,
    s_tab, r_tab, s_w, r_w, s_x, r_x, s_hf, r_hf, s_hb, r_hb, s_red, r_red, s_g, r_g,
):
    s = lax.axis_index("section")
    e = lax.axis_index("dp")
    h, z = lax.rem(s, 2), lax.div(s, 2)
    c, q = lax.rem(e, 2), lax.div(e, 2)
    chip = h * 8 + q
    owner_core = lax.div(e, 8)
    local = c == owner_core
    other = (s, e + 1 - 2 * c)

    barrier = pltpu.get_barrier_semaphore()

    def greet(t, carry):
        place = lax.rem(h * 16 + e + t, 32)
        pl.semaphore_signal(
            barrier, inc=1, device_id=(2 * z + lax.div(place, 16), lax.rem(place, 16)), device_id_type=MESH
        )
        return carry

    lax.fori_loop(1, 32, greet, 0)

    @pl.when(z > 0)
    def _():
        pl.semaphore_signal(barrier, inc=1, device_id=(s - 2, e), device_id_type=MESH)

    @pl.when(z < STAGES - 1)
    def _():
        pl.semaphore_signal(barrier, inc=1, device_id=(s + 2, e), device_id_type=MESH)

    neighbours = jnp.where(z > 0, 1, 0) + jnp.where(z < STAGES - 1, 1, 0)
    pl.semaphore_wait(barrier, 31 + neighbours)

    def table_copy(which, k, t, first=False):
        src = ((rec_in, sent_in), (tok_in, cot_in))[first][which]
        dst = (rec, sent)[which]
        h2, c2 = lax.rem(h + t // 2, 2), lax.rem(c + t, 2)
        row = pl.multiple_of((2 * k + c) * TOK, TOK)
        return dict(
            src_ref=src.at[4 * h2 + k, :, pl.ds(pl.multiple_of(c2 * HALF, HALF), HALF)],
            dst_ref=dst.at[h, pl.ds(row, TOK), :],
        ), s_tab.at[which, k, t], r_tab.at[which, h, 2 * k + c], (2 * z + h2, 2 * q + c2)

    def table_start(which, k):
        end = s == (0, 2 * STAGES - 1)[which]

        def start(first):
            for t in range(4):
                refs, ssem, rsem, dev = table_copy(which, k, t, first)
                if t == 0:
                    pltpu.make_async_copy(refs["src_ref"], refs["dst_ref"], rsem).start()
                else:
                    pltpu.make_async_remote_copy(
                        **refs, send_sem=ssem, recv_sem=rsem, device_id=dev, device_id_type=MESH
                    ).start()

        @pl.when(end)
        def _():
            start(True)

        @pl.when(jnp.logical_not(end))
        def _():
            start(False)

    def table_sent(which, k):
        for t in range(1, 4):
            refs, ssem, rsem, dev = table_copy(which, k, t)
            pltpu.make_async_remote_copy(
                **refs, send_sem=ssem, recv_sem=rsem, device_id=dev, device_id_type=MESH
            ).wait_send()

    def table_wait(which, part, i):
        place = (rec, sent)[which].at[part, pl.ds(pl.multiple_of(i * TOK, TOK), TOK), :]
        pltpu.make_async_copy(place, place, r_tab.at[which, part, i]).wait()

    slot = lax.rem(e, 8)
    spot = pl.multiple_of(slot * CH, CH)
    col_x = lax.rem(q, 4)
    wide = pl.ds(pl.multiple_of(col_x * 2 * CH, 2 * CH), 2 * CH)

    def shard_refs(kind):
        if kind == 0:
            return down_in, wd.at[h, pl.ds(spot, CH), :]
        return up_in, wu.at[h, :, pl.ds(spot, CH)]

    def shard_remote(kind, t):
        src, dst = shard_refs(kind)
        y = lax.rem(2 * h + owner_core + t, 4)
        return pltpu.make_async_remote_copy(
            src_ref=src, dst_ref=dst, send_sem=s_w.at[kind, t], recv_sem=r_w.at[kind, h, lax.rem(e, 2)],
            device_id=(2 * z + lax.div(y, 2), 8 * lax.rem(y, 2) + 2 * col_x + owner_core), device_id_type=MESH,
        )

    def shard_start(kind):
        @pl.when(local)
        def _():
            src, dst = shard_refs(kind)
            pltpu.make_async_copy(src, dst, r_w.at[kind, h, lax.rem(e, 2)]).start()

        @pl.when(jnp.logical_not(local))
        def _():
            shard_remote(kind, 0).start()

        for t in range(1, 4):
            shard_remote(kind, t).start()

    def shard_sent(kind):
        @pl.when(jnp.logical_not(local))
        def _():
            shard_remote(kind, 0).wait_send()

        for t in range(1, 4):
            shard_remote(kind, t).wait_send()

    def shard_wait(kind, part):
        for j in range(2):
            at = pl.ds(pl.multiple_of((2 * col_x + j) * CH, CH), CH)
            place = wd.at[part, at, :] if kind == 0 else wu.at[part, :, at]
            pltpu.make_async_copy(place, place, r_w.at[kind, part, j]).wait()

    def block(kind, part, at):
        return wd.at[part, at, :] if kind == 0 else wu.at[part, :, at]

    def block_copy(kind, part, t):
        place = block(kind, part, wide)
        return pltpu.make_async_remote_copy(
            src_ref=place, dst_ref=place, send_sem=s_x.at[kind, part, t], recv_sem=r_x.at[kind, part, col_x],
            device_id=(s, e - 2 * col_x + 2 * lax.rem(col_x + t, 4)), device_id_type=MESH,
        )

    def block_start(kind, part):
        shard_wait(kind, part)
        for t in (1, 3, 2):
            block_copy(kind, part, t).start()

    def weight_wait(kind, part):
        for t in range(1, 4):
            x = lax.rem(col_x + t, 4)
            place = block(kind, part, pl.ds(pl.multiple_of(x * 2 * CH, 2 * CH), 2 * CH))
            pltpu.make_async_copy(place, place, r_x.at[kind, part, x]).wait()

    def weight_sent(kind):
        shard_sent(kind)
        for part in range(2):
            for t in range(1, 4):
                block_copy(kind, part, t).wait_send()

    shard_start(0)
    table_start(0, 0)
    shard_start(1)
    table_start(1, 0)
    for part in range(2):
        for kind in range(2):
            block_start(kind, part)
    for k in range(1, 4):
        table_start(0, k)
        table_start(1, k)

    def red_copy(n):
        return pltpu.make_async_remote_copy(
            src_ref=red_tx.at[n], dst_ref=red_rx.at[n], send_sem=s_red.at[n], recv_sem=r_red.at[n],
            device_id=other, device_id_type=MESH,
        )

    def col(n):
        return slice(n * COLS, (n + 1) * COLS)

    def hop(n, i, ahead):
        at = (slice(None), col(n))
        if ahead:
            buf, dst, ss, rs, dev = fout, xin, s_hf, r_hf, (s + 2, e)
        else:
            buf, dst, ss, rs, dev = bout, uin, s_hb, r_hb, (s - 2, e)
        rows = pl.ds(pl.multiple_of(i * TOK, TOK), TOK)
        return pltpu.make_async_remote_copy(
            src_ref=buf.at[rows, col(n)], dst_ref=dst.at[rows, col(n)], send_sem=ss.at[i, n], recv_sem=rs.at[i, n],
            device_id=dev, device_id_type=MESH,
        )

    def rows_refs(kind, part, b, j):
        at = pl.ds(b * BROWS, BROWS)
        feat = pl.ds(pl.multiple_of(j * CH, CH), CH)
        if kind == 0:
            return xs.at[part, at, feat]
        if kind == 1:
            return act.at[part, at, :]
        if kind == 2:
            return vee.at[part, at, :]
        return (um, uin)[part].at[at, feat]

    def rows_copy(kind, b, part, j):
        dst = (gx, ga, gv, gw)[kind].at[b, pl.ds(pl.multiple_of(chip * BROWS, BROWS), BROWS), :]
        return rows_refs(kind, part, b, j), dst, s_g.at[kind, b, part, j], r_g.at[kind, b, chip], (2 * z + part, 8 * c + j)

    def rows_each(kind, b, own, far):
        for part in range(2):
            def one(t, carry):
                j = lax.rem(q + t, 8)
                src, dst, ssem, rsem, dev = rows_copy(kind, b, part, j)
                mine = jnp.logical_and(h == part, 8 * c + j == e)
                remote = pltpu.make_async_remote_copy(
                    src_ref=src, dst_ref=dst, send_sem=ssem, recv_sem=rsem, device_id=dev, device_id_type=MESH
                )
                if own:
                    @pl.when(mine)
                    def _():
                        pltpu.make_async_copy(src, dst, rsem).start()

                @pl.when(jnp.logical_not(mine))
                def _():
                    far(remote)

                return carry

            lax.fori_loop(0, 8, one, 0)

    def rows_start(kind, b):
        rows_each(kind, b, True, lambda copy: copy.start())

    def rows_sent(kind, b):
        rows_each(kind, b, False, lambda copy: copy.wait_send())

    def rows_wait(kind, b):
        def one(t, carry):
            place = (gx, ga, gv, gw)[kind].at[b, pl.ds(pl.multiple_of(t * BROWS, BROWS), BROWS), :]
            pltpu.make_async_copy(place, place, r_g.at[kind, b, t]).wait()
            return carry

        lax.fori_loop(0, 16, one, 0)

    def forward(i, carry):
        rows = pl.ds(pl.multiple_of(i * TOK, TOK), TOK)
        table_wait(0, 0, i)

        @pl.when(i == 0)
        def _():
            weight_wait(0, 0)

        acc = jnp.zeros((TOK, RANK), F32)
        sq = jnp.zeros((TOK, 128), F32)
        for n in range(NCOL):
            @pl.when(z > 0)
            def _():
                hop(n, i, True).wait_recv()
                xf[:, col(n)] = rec[0, rows, col(n)].astype(F32) + xin[rows, col(n)].astype(F32)

            @pl.when(z == 0)
            def _():
                xf[:, col(n)] = rec[0, rows, col(n)].astype(F32)

            x = xf[:, col(n)]
            xb = x.astype(BF16)
            xs[0, rows, col(n)] = xb
            sq = sq + lanes(x * x)
            acc = acc + nn(xb, wd[0, col(n), :])

        def finish(part, acc, sq):
            n = 2 * i + part
            red_tx[n, :, 0:RANK] = acc
            red_tx[n, :, RANK:] = sq
            red_copy(n).start()
            red_copy(n).wait_recv()
            total = acc + red_rx[n, :, 0:RANK]
            square = jnp.sum(sq + red_rx[n, :, RANK:], axis=1, keepdims=True)
            scale = lax.rsqrt(square * (1.0 / D) + EPS)
            v = total * scale
            pre[part, rows, :] = v
            scl[part, rows, :] = jnp.broadcast_to(scale, (TOK, 128))
            a = (v * jax.nn.sigmoid(v)).astype(BF16)
            act[part, rows, :] = a
            return a

        a = finish(0, acc, sq)

        @pl.when(i == 0)
        def _():
            weight_wait(1, 0)
            weight_wait(0, 1)

        table_wait(0, 1, i)
        table_wait(1, 0, i)
        acc = jnp.zeros((TOK, RANK), F32)
        sq = jnp.zeros((TOK, 128), F32)
        for n in range(NCOL):
            x = (
                xf[:, col(n)] + nn(a, wu[0, :, col(n)])
                + (rec[1, rows, col(n)].astype(F32) - sent[0, rows, col(n)].astype(F32))
            )
            xf[:, col(n)] = x
            xb = x.astype(BF16)
            xs[1, rows, col(n)] = xb
            sq = sq + lanes(x * x)
            acc = acc + nn(xb, wd[1, col(n), :])
        a = finish(1, acc, sq)

        @pl.when(i == 0)
        def _():
            weight_wait(1, 1)

        table_wait(1, 1, i)

        @pl.when(z < STAGES - 1)
        def _():
            for n in range(NCOL):
                x = xf[:, col(n)] + nn(a, wu[1, :, col(n)]) - sent[1, rows, col(n)].astype(F32)
                fout[rows, col(n)] = x.astype(BF16)
                hop(n, i, True).start()

        return carry

    lax.fori_loop(0, MB, forward, 0)

    def early():
        for b in range(BATCHES):
            rows_start(0, b)
            rows_start(1, b)

    @pl.when(z < STAGES - 1)
    def _():
        early()

    def backward(i, carry):
        rows = pl.ds(pl.multiple_of(i * TOK, TOK), TOK)
        acc = jnp.zeros((TOK, RANK), F32)
        for n in range(NCOL):
            @pl.when(z < STAGES - 1)
            def _():
                hop(n, i, False).wait_recv()

            @pl.when(z == STAGES - 1)
            def _():
                uin[rows, col(n)] = sent[1, rows, col(n)]

            acc = acc + nt(uin[rows, col(n)], wu[1, :, col(n)])

        def finish(part, acc):
            n = 2 * MB + 2 * i + part
            red_tx[n, :, 0:RANK] = acc
            red_tx[n, :, RANK:] = jnp.zeros((TOK, 128), F32)
            red_copy(n).start()
            red_copy(n).wait_recv()
            total = acc + red_rx[n, :, 0:RANK]
            v = pre[part, rows, :]
            gate = jax.nn.sigmoid(v)
            d_pre = total * gate * (1.0 + v * (1.0 - gate))
            scale = scl[part, rows, 0:1]
            mean = jnp.sum(d_pre * v, axis=1, keepdims=True) * (1.0 / D)
            back = (d_pre * scale).astype(BF16)
            vee[part, rows, :] = back
            return back, mean * scale * scale

        back, shrink = finish(1, acc)
        acc = jnp.zeros((TOK, RANK), F32)
        for n in range(NCOL):
            u = (
                uin[rows, col(n)].astype(F32) + nt(back, wd[1, col(n), :])
                - shrink * xs[1, rows, col(n)].astype(F32)
            ).astype(BF16)
            um[rows, col(n)] = u
            acc = acc + nt(u, wu[0, :, col(n)])
        back, shrink = finish(0, acc)

        @pl.when(z > 0)
        def _():
            for n in range(NCOL):
                u = (
                    um[rows, col(n)].astype(F32) + nt(back, wd[0, col(n), :])
                    - shrink * xs[0, rows, col(n)].astype(F32)
                )
                bout[rows, col(n)] = u.astype(BF16)
                hop(n, i, False).start()

        return carry

    for b in range(BATCHES):
        lax.fori_loop(b * MB // BATCHES, (b + 1) * MB // BATCHES, backward, 0)
        rows_start(2, b)
        rows_start(3, b)

    @pl.when(z == STAGES - 1)
    def _():
        early()

    def total(b):
        def one(n, carry):
            at = pl.ds(pl.multiple_of(n * 256, 256), 256)
            gd_out[...] += tn(gx[b, at, :], gv[b, at, :])
            gu_out[...] += tn(ga[b, at, :], gw[b, at, :])
            return carry

        lax.fori_loop(0, 16 * BROWS // 256, one, 0)

    gd_out[...] = jnp.zeros_like(gd_out)
    gu_out[...] = jnp.zeros_like(gu_out)
    for b in range(BATCHES):
        for kind in range(4):
            rows_wait(kind, b)
        total(b)

    for b in range(BATCHES):
        for kind in range(4):
            rows_sent(kind, b)
    weight_sent(0)
    weight_sent(1)
    for k in range(4):
        table_sent(0, k)
        table_sent(1, k)

    def rest(i, carry):
        for n in range(NCOL):
            @pl.when(z < STAGES - 1)
            def _():
                hop(n, i, True).wait_send()

            @pl.when(z > 0)
            def _():
                hop(n, i, False).wait_send()

        for k in range(4):
            red_copy(4 * i + k).wait_send()
        return carry

    lax.fori_loop(0, MB, rest, 0)


def shards(tokens, cotangent, sample_ids, sent_before, received_before, norm_gain, down_proj, up_proj):
    e = lax.axis_index("dp")
    ids = sample_ids[0]
    micro = jnp.arange(MB, dtype=jnp.int32)
    where_is = jnp.sum(jnp.where(ids[None, :] == micro[:, None], micro[None, :], 0), axis=1)
    tok = jnp.take(tokens, where_is, axis=0, mode="clip")
    cot = jnp.take(cotangent, where_is, axis=0, mode="clip")
    gain = lax.dynamic_slice(norm_gain[0], (e * CH,), (CH,))[:, None]
    down = (down_proj[0].astype(F32) * gain).astype(BF16)
    any_ = pl.BlockSpec(memory_space=pl.ANY)
    vmem = pl.BlockSpec(memory_space=pltpu.VMEM)
    dma = pltpu.SemaphoreType.DMA
    rows = MB * TOK
    grad_down, grad_up = pl.pallas_call(
        kernel,
        out_shape=(jax.ShapeDtypeStruct((CH, RANK), F32), jax.ShapeDtypeStruct((RANK, CH), F32)),
        in_specs=[any_] * 6,
        out_specs=(vmem, vmem),
        scratch_shapes=[
            pltpu.VMEM((2, rows, HALF), BF16),
            pltpu.VMEM((2, rows, HALF), BF16),
            pltpu.VMEM((2, HALF, RANK), BF16),
            pltpu.VMEM((2, RANK, HALF), BF16),
            pltpu.VMEM((rows, HALF), BF16),
            pltpu.VMEM((rows, HALF), BF16),
            pltpu.VMEM((2, rows, HALF), BF16),
            pltpu.VMEM((rows, HALF), BF16),
            pltpu.VMEM((TOK, HALF), F32),
            pltpu.VMEM((rows, HALF), BF16),
            pltpu.VMEM((rows, HALF), BF16),
            pltpu.VMEM((4 * MB, TOK, RANK + 128), F32),
            pltpu.VMEM((4 * MB, TOK, RANK + 128), F32),
            pltpu.VMEM((2, rows, RANK), F32),
            pltpu.VMEM((2, rows, RANK), BF16),
            pltpu.VMEM((2, rows, RANK), BF16),
            pltpu.VMEM((2, rows, 128), F32),
            pltpu.VMEM((BATCHES, 16 * BROWS, CH), BF16),
            pltpu.VMEM((BATCHES, 16 * BROWS, RANK), BF16),
            pltpu.VMEM((BATCHES, 16 * BROWS, RANK), BF16),
            pltpu.VMEM((BATCHES, 16 * BROWS, CH), BF16),
            dma((2, 4, 4)), dma((2, 2, MB)),
            dma((2, 4)), dma((2, 2, 2)),
            dma((2, 2, 4)), dma((2, 2, 4)),
            dma((MB, NCOL)), dma((MB, NCOL)),
            dma((MB, NCOL)), dma((MB, NCOL)),
            dma((4 * MB,)), dma((4 * MB,)),
            dma((4, BATCHES, 2, 8)), dma((4, BATCHES, 16)),
        ],
        compiler_params=pltpu.CompilerParams(
            collective_id=0, has_side_effects=True, vmem_limit_bytes=56 * 1024 * 1024
        ),
    )(received_before[0], sent_before[0], tok, cot, down, up_proj[0])
    return ((grad_down * gain)[None], grad_up[None])


def solution(mesh):
    placed = (
        P(None, "dp", None),
        P(None, "dp", None),
        P("dp", None),
        P("section", "dp", None, None),
        P("section", "dp", None, None),
        P("section", None),
        P("section", "dp", None),
        P("section", None, "dp"),
    )
    return jax.shard_map(
        shards,
        mesh=mesh,
        in_specs=placed,
        out_specs=(P("section", "dp", None), P("section", None, "dp")),
        check_vma=False,
    )
```

```python
import functools

import jax
import jax.numpy as jnp
from jax import lax
from jax.experimental import pallas as pl
from jax.experimental.pallas import tpu as pltpu
from jax.sharding import PartitionSpec as P

MESH = pl.DeviceIdType.MESH
F32, BF16 = jnp.float32, jnp.bfloat16
EPS = 1e-05
D = 8192
HALF = 4096
RANK = 256
TOK = 16
MB = 8
CH = 512
COLS = 512
NCOL = HALF // COLS
STAGES = 8
BATCH = 2 * TOK
NBATCH = MB * TOK // BATCH
PACK = CH + RANK


def tn(a, b):
    return lax.dot_general(a, b, (((0,), (0,)), ((), ())), preferred_element_type=F32)


def nn(a, b):
    return jnp.dot(a, b, preferred_element_type=F32)


def lanes(v):
    total = v[:, 0:128]
    for k in range(128, v.shape[1], 128):
        total = total + v[:, k : k + 128]
    return total


def kernel(
    ids, rec_in, sent_in, tok_in, cot_in, gain_in, down_in, up_in, gd_out, gu_out,
    raw, perm, gn, rec, sent, wd, wu, wdt, wut, xin, xz, uz, xf, fout, bout, red_tx, red_rx,
    pre, scl, gxz, guz,
    c_raw, s_tok, s_gn, r_gn, s_tab, r_tab, s_w, r_w, s_x, r_x, s_xr, r_xr,
    s_u, r_u, s_v, r_v, s_vr, r_vr,
    s_hf, r_hf, s_hb, r_hb, s_red, r_red, s_g, r_g,
):
    s = lax.axis_index("section")
    e = lax.axis_index("dp")
    h, z = lax.rem(s, 2), lax.div(s, 2)
    c, q = lax.rem(e, 2), lax.div(e, 2)
    chip = h * 8 + q
    owner_core = lax.div(e, 8)
    local = c == owner_core
    other = (s, e + 1 - 2 * c)

    raw_tok = pltpu.make_async_copy(tok_in, raw, c_raw)
    raw_cot = pltpu.make_async_copy(cot_in, raw, c_raw)

    @pl.when(z == 0)
    def _():
        raw_tok.start()

    @pl.when(z == STAGES - 1)
    def _():
        raw_cot.start()

    barrier = pltpu.get_barrier_semaphore()

    def greet(t, carry):
        place = lax.rem(h * 16 + e + t, 32)
        pl.semaphore_signal(
            barrier, inc=1, device_id=(2 * z + lax.div(place, 16), lax.rem(place, 16)), device_id_type=MESH
        )
        return carry

    lax.fori_loop(1, 32, greet, 0)

    @pl.when(z > 0)
    def _():
        pl.semaphore_signal(barrier, inc=1, device_id=(s - 2, e), device_id_type=MESH)

    @pl.when(z < STAGES - 1)
    def _():
        pl.semaphore_signal(barrier, inc=1, device_id=(s + 2, e), device_id_type=MESH)

    neighbours = jnp.where(z > 0, 1, 0) + jnp.where(z < STAGES - 1, 1, 0)
    pl.semaphore_wait(barrier, 31 + neighbours)

    def table_copy(which, k, t):
        src = (rec_in, sent_in)[which]
        dst = (rec, sent)[which]
        h2, c2 = lax.rem(h + t // 2, 2), lax.rem(c + t, 2)
        row = pl.multiple_of((2 * k + c) * TOK, TOK)
        return dict(
            src_ref=src.at[4 * h2 + k, :, pl.ds(pl.multiple_of(c2 * HALF, HALF), HALF)],
            dst_ref=dst.at[h, pl.ds(row, TOK), :],
        ), s_tab.at[which, k, t], r_tab.at[which, h, 2 * k + c], (2 * z + h2, 2 * q + c2)

    def table_used(which):
        return s != (0, 2 * STAGES - 1)[which]

    def table_start(which, k):
        @pl.when(table_used(which))
        def _():
            for t in range(4):
                refs, ssem, rsem, dev = table_copy(which, k, t)
                if t == 0:
                    pltpu.make_async_copy(refs["src_ref"], refs["dst_ref"], rsem).start()
                else:
                    pltpu.make_async_remote_copy(
                        **refs, send_sem=ssem, recv_sem=rsem, device_id=dev, device_id_type=MESH
                    ).start()

    def table_sent(which, k):
        @pl.when(table_used(which))
        def _():
            for t in range(1, 4):
                refs, ssem, rsem, dev = table_copy(which, k, t)
                pltpu.make_async_remote_copy(
                    **refs, send_sem=ssem, recv_sem=rsem, device_id=dev, device_id_type=MESH
                ).wait_send()

    def end_copies(which, k):
        dst, part = ((rec, 0), (sent, 1))[which]
        place = dst.at[part, pl.ds(pl.multiple_of((2 * k + c) * TOK, TOK), TOK), :]
        rsem = r_tab.at[which, part, 2 * k + c]
        mine = perm.at[k, :, pl.ds(pl.multiple_of(c * HALF, HALF), HALF)]
        return mine, place, rsem

    def end_far(which, k):
        theirs = perm.at[k, :, pl.ds(pl.multiple_of((1 - c) * HALF, HALF), HALF)]
        place, rsem = end_copies(which, k)[1:]
        return pltpu.make_async_remote_copy(
            src_ref=theirs, dst_ref=place, send_sem=s_tok.at[k], recv_sem=rsem, device_id=other, device_id_type=MESH
        )

    def end_start(which):
        (raw_tok, raw_cot)[which].wait()
        for k in range(4):
            at = jnp.int32(0)
            for m in range(1, MB):
                at = jnp.where(ids[0, m] == 4 * h + k, m, at)
            at = jnp.clip(at, 0, MB - 1)

            def move(n, carry, at=at, k=k):
                cols = pl.ds(pl.multiple_of(n * 1024, 1024), 1024)
                perm[k, :, cols] = raw[at, :, cols]
                return carry

            lax.fori_loop(0, D // 1024, move, 0)
            end_far(which, k).start()
            pltpu.make_async_copy(*end_copies(which, k)).start()

    def end_sent(which):
        for k in range(4):
            end_far(which, k).wait_send()

    def table_wait(which, part, i):
        place = (rec, sent)[which].at[part, pl.ds(pl.multiple_of(i * TOK, TOK), TOK), :]
        pltpu.make_async_copy(place, place, r_tab.at[which, part, i]).wait()

    slot = lax.rem(e, 8)
    spot = pl.ds(pl.multiple_of(slot * CH, CH), CH)
    col_x = lax.rem(q, 4)
    row_y = 2 * h + owner_core

    def device(x, y, core):
        return (2 * z + lax.div(y, 2), 8 * lax.rem(y, 2) + 2 * x + core)

    def wide(x):
        return pl.ds(pl.multiple_of(x * 2 * CH, 2 * CH), 2 * CH)

    def away(t):
        return lax.rem(col_x + t, 4)

    def w_remote(t):
        return pltpu.make_async_remote_copy(
            src_ref=down_in, dst_ref=wd.at[h, spot, :], send_sem=s_w.at[t], recv_sem=r_w.at[h, c],
            device_id=device(col_x, lax.rem(row_y + t, 4), owner_core), device_id_type=MESH,
        )

    def u_remote(t):
        return pltpu.make_async_remote_copy(
            src_ref=up_in, dst_ref=wu.at[h, :, spot], send_sem=s_u.at[t], recv_sem=r_u.at[slot],
            device_id=device(away(t), row_y, owner_core), device_id_type=MESH,
        )

    def first_start():
        @pl.when(local)
        def _():
            pltpu.make_async_copy(down_in, wd.at[h, spot, :], r_w.at[h, c]).start()

        @pl.when(jnp.logical_not(local))
        def _():
            w_remote(0).start()

        for t in (1, 3, 2):
            w_remote(t).start()

        @pl.when(local)
        def _():
            pltpu.make_async_copy(up_in, wu.at[h, :, spot], r_u.at[slot]).start()

        @pl.when(jnp.logical_not(local))
        def _():
            u_remote(0).start()

        for t in (1, 3, 2):
            u_remote(t).start()

    def first_sent():
        @pl.when(jnp.logical_not(local))
        def _():
            w_remote(0).wait_send()
            u_remote(0).wait_send()

        for t in range(1, 4):
            w_remote(t).wait_send()
            u_remote(t).wait_send()

    def w_block(part, t):
        place = wd.at[part, wide(col_x), :]
        return pltpu.make_async_remote_copy(
            src_ref=place, dst_ref=place, send_sem=s_x.at[part, t], recv_sem=r_x.at[part, col_x],
            device_id=(s, e - 2 * col_x + 2 * away(t)), device_id_type=MESH,
        )

    def w_start(part):
        for j in range(2):
            place = wd.at[part, pl.ds(pl.multiple_of((2 * col_x + j) * CH, CH), CH), :]
            pltpu.make_async_copy(place, place, r_w.at[part, j]).wait()
        for t in (1, 3):
            w_block(part, t).start()

    def w_half(part, x, half):
        return wd.at[part, pl.ds(pl.multiple_of((2 * x + half) * CH, CH), CH), :]

    def w_relay(part, half):
        place = w_half(part, away((3, 1)[half]), half)
        return pltpu.make_async_remote_copy(
            src_ref=place, dst_ref=place, send_sem=s_xr.at[part, half], recv_sem=r_xr.at[part, half],
            device_id=(s, e - 2 * col_x + 2 * away((1, 3)[half])), device_id_type=MESH,
        )

    def w_forward(part):
        for half in range(2):
            x = away((3, 1)[half])
            place = wd.at[part, wide(x), :]
            pltpu.make_async_copy(place, place, r_x.at[part, x]).wait()
            w_relay(part, half).start()

    def u_block(n, t):
        place = wu.at[h, :, wide(away(n))]
        return pltpu.make_async_remote_copy(
            src_ref=place, dst_ref=place, send_sem=s_v.at[n, t], recv_sem=r_v.at[h, away(n)],
            device_id=device(col_x, lax.rem(row_y + t, 4), c), device_id_type=MESH,
        )

    def u_start(n):
        @pl.when(local)
        def _():
            for j in range(2):
                at = 2 * away(n) + j
                place = wu.at[h, :, pl.ds(pl.multiple_of(at * CH, CH), CH)]
                pltpu.make_async_copy(place, place, r_u.at[at]).wait()
            for t in (1, 3):
                u_block(n, t).start()

    y_me = 2 * h + lax.div(e, 8)

    def u_half(part, n, half):
        return wu.at[part, pl.ds(pl.multiple_of(half * (RANK // 2), RANK // 2), RANK // 2), wide(away(n))]

    def u_relay(part, n):
        half = jnp.where(lax.rem(y_me - 2 * part - c + 4, 4) == 1, 0, 1)
        place = u_half(part, n, half)
        return pltpu.make_async_remote_copy(
            src_ref=place, dst_ref=place, send_sem=s_vr.at[part, n], recv_sem=r_vr.at[n, half],
            device_id=device(col_x, lax.rem(y_me + 1 + 2 * half, 4), c), device_id_type=MESH,
        )

    def u_forward(n):
        @pl.when(jnp.logical_not(local))
        def _():
            for part in range(2):
                place = wu.at[part, :, wide(away(n))]
                pltpu.make_async_copy(place, place, r_v.at[part, away(n)]).wait()
                u_relay(part, n).start()

    def weight_wait(kind, part):
        if kind == 0:
            for half in range(2):
                place = w_half(part, away(2), half)
                pltpu.make_async_copy(place, place, r_xr.at[part, half]).wait()
        else:
            @pl.when(jnp.logical_and(local, h != part))
            def _():
                for n in range(4):
                    for half in range(2):
                        place = u_half(part, n, half)
                        pltpu.make_async_copy(place, place, r_vr.at[n, half]).wait()

    def weight_sent():
        first_sent()
        for part in range(2):
            for t in (1, 3):
                w_block(part, t).wait_send()
            for half in range(2):
                w_relay(part, half).wait_send()

        @pl.when(local)
        def _():
            for n in range(4):
                for t in (1, 3):
                    u_block(n, t).wait_send()

        @pl.when(jnp.logical_not(local))
        def _():
            for n in range(4):
                for part in range(2):
                    u_relay(part, n).wait_send()

    gain_part = gain_in.at[:, pl.ds(pl.multiple_of(c * HALF, HALF), HALF)]
    gain_near = pltpu.make_async_copy(gain_part, gn.at[h], r_gn.at[h])
    gain_far = pltpu.make_async_remote_copy(
        src_ref=gain_part, dst_ref=gn.at[h], send_sem=s_gn, recv_sem=r_gn.at[h],
        device_id=(s + 1 - 2 * h, e), device_id_type=MESH,
    )

    first_start()
    gain_near.start()
    gain_far.start()
    table_start(0, 0)
    table_start(1, 0)

    @pl.when(z == 0)
    def _():
        end_start(0)

    @pl.when(z == STAGES - 1)
    def _():
        end_start(1)

    w_start(0)
    u_start(0)
    w_start(1)
    for n in (1, 3, 2):
        u_start(n)
    w_forward(0)
    u_forward(0)
    w_forward(1)
    u_forward(1)
    u_forward(3)
    table_start(0, 1)
    table_start(1, 1)
    u_forward(2)
    for k in range(2, 4):
        table_start(0, k)
        table_start(1, k)
    for part in range(2):
        pltpu.make_async_copy(gn.at[part], gn.at[part], r_gn.at[part]).wait()

    def red_copy(n):
        return pltpu.make_async_remote_copy(
            src_ref=red_tx.at[n], dst_ref=red_rx.at[n], send_sem=s_red.at[n], recv_sem=r_red.at[n],
            device_id=other, device_id_type=MESH,
        )

    def col(n):
        return slice(n * COLS, (n + 1) * COLS)

    def hop(n, i, ahead):
        rows = pl.ds(pl.multiple_of(i * TOK, TOK), TOK)
        if ahead:
            wide_col = slice(2 * n * COLS, 2 * (n + 1) * COLS)
            src, dst, ss, rs, dev = fout.at[rows, wide_col], xin.at[rows, wide_col], s_hf, r_hf, (s + 2, e)
        else:
            two = pl.ds(2 * n, 2)
            src, dst, ss, rs, dev = bout.at[two, rows, :], uz.at[1, two, rows, pl.ds(0, CH)], s_hb, r_hb, (s - 2, e)
        return pltpu.make_async_remote_copy(
            src_ref=src, dst_ref=dst, send_sem=ss.at[i, n], recv_sem=rs.at[i, n], device_id=dev, device_id_type=MESH
        )

    def rows_copy(kind, b, part, j):
        src = (xz, uz)[kind].at[part, j, pl.ds(pl.multiple_of(b * BATCH, BATCH), BATCH), :]
        return src, landing(kind, b, chip), s_g.at[kind, b, part, j], r_g.at[kind, b, chip], (2 * z + part, 8 * c + j)

    def landing(kind, b, source):
        at = pl.ds(pl.multiple_of((16 * b + source) * BATCH, BATCH), BATCH)
        return (gxz, guz)[kind].at[at, :]

    def rows_each(kind, b, own, far):
        def one(t, carry):
            place = lax.rem(chip + t, 16)
            part, j = lax.div(place, 8), lax.rem(place, 8)
            src, dst, ssem, rsem, dev = rows_copy(kind, b, part, j)
            mine = jnp.logical_and(h == part, 8 * c + j == e)
            if own:
                @pl.when(mine)
                def _():
                    pltpu.make_async_copy(src, dst, rsem).start()

            @pl.when(jnp.logical_not(mine))
            def _():
                far(
                    pltpu.make_async_remote_copy(
                        src_ref=src, dst_ref=dst, send_sem=ssem, recv_sem=rsem, device_id=dev, device_id_type=MESH
                    )
                )

            return carry

        lax.fori_loop(0, 16, one, 0)

    def rows_start(kind, b):
        rows_each(kind, b, True, lambda copy: copy.start())

    def rows_sent(kind, b):
        rows_each(kind, b, False, lambda copy: copy.wait_send())

    def rows_wait(kind, b):
        def one(t, carry):
            place = landing(kind, b, t)
            pltpu.make_async_copy(place, place, r_g.at[kind, b, t]).wait()
            return carry

        lax.fori_loop(0, 16, one, 0)

    def turn():
        for part in range(2):
            def one(j, carry, part=part):
                at = pl.ds(pl.multiple_of(j * CH, CH), CH)
                wdt[part, :, at] = wd[part, at, :].T
                wut[part, at, :] = wu[part, :, at].T
                return carry

            lax.fori_loop(0, HALF // CH, one, 0)

    late = z >= STAGES // 2

    @pl.when(late)
    def _():
        for kind in range(2):
            for part in range(2):
                weight_wait(kind, part)
        turn()

    def forward(i, carry):
        rows = pl.ds(pl.multiple_of(i * TOK, TOK), TOK)
        fresh = jnp.logical_and(i == 0, jnp.logical_not(late))
        table_wait(0, 0, i)

        @pl.when(fresh)
        def _():
            weight_wait(0, 0)

        acc = jnp.zeros((TOK, RANK), F32)
        sq = jnp.zeros((TOK, 128), F32)
        for n in range(NCOL):
            @pl.when(z > 0)
            def _():
                if n % 2 == 0:
                    hop(n // 2, i, True).wait_recv()
                xf[:, col(n)] = rec[0, rows, col(n)].astype(F32) + xin[rows, col(n)].astype(F32)

            @pl.when(z == 0)
            def _():
                xf[:, col(n)] = rec[0, rows, col(n)].astype(F32)

            x = xf[:, col(n)]
            xz[0, n, rows, 0:CH] = x.astype(BF16)
            sq = sq + lanes(x * x)
            acc = acc + nn((x * gn[0, :, col(n)]).astype(BF16), wd[0, col(n), :])

        def finish(part, acc, sq):
            n = 2 * i + part
            red_tx[n, :, 0:RANK] = acc
            red_tx[n, :, RANK:] = sq
            red_copy(n).start()
            red_copy(n).wait_recv()
            total = acc + red_rx[n, :, 0:RANK]
            square = jnp.sum(sq + red_rx[n, :, RANK:], axis=1, keepdims=True)
            scale = lax.rsqrt(square * (1.0 / D) + EPS)
            v = total * scale
            pre[part, rows, :] = v
            scl[part, rows, :] = jnp.broadcast_to(scale, (TOK, 128))
            a = (v * jax.nn.sigmoid(v)).astype(BF16)
            for j in range(8):
                xz[part, j, rows, CH:] = a
            return a

        a = finish(0, acc, sq)

        @pl.when(fresh)
        def _():
            weight_wait(1, 0)
            weight_wait(0, 1)

        table_wait(0, 1, i)
        table_wait(1, 0, i)
        acc = jnp.zeros((TOK, RANK), F32)
        sq = jnp.zeros((TOK, 128), F32)
        for n in range(NCOL):
            x = (
                xf[:, col(n)] + nn(a, wu[0, :, col(n)])
                + (rec[1, rows, col(n)].astype(F32) - sent[0, rows, col(n)].astype(F32))
            )
            xf[:, col(n)] = x
            xz[1, n, rows, 0:CH] = x.astype(BF16)
            sq = sq + lanes(x * x)
            acc = acc + nn((x * gn[1, :, col(n)]).astype(BF16), wd[1, col(n), :])
        a = finish(1, acc, sq)

        @pl.when(fresh)
        def _():
            weight_wait(1, 1)

        table_wait(1, 1, i)

        @pl.when(z < STAGES - 1)
        def _():
            for n in range(NCOL):
                x = xf[:, col(n)] + nn(a, wu[1, :, col(n)]) - sent[1, rows, col(n)].astype(F32)
                fout[rows, col(n)] = x.astype(BF16)
                if n % 2 == 1:
                    hop(n // 2, i, True).start()

        return carry

    lax.fori_loop(0, MB, forward, 0)

    @pl.when(jnp.logical_not(late))
    def _():
        turn()

    def early():
        def one(b, carry):
            rows_start(0, b)
            return carry

        lax.fori_loop(0, NBATCH, one, 0)

    @pl.when(z < STAGES - 1)
    def _():
        early()

    def backward(i, carry):
        rows = pl.ds(pl.multiple_of(i * TOK, TOK), TOK)
        acc = jnp.zeros((TOK, RANK), F32)
        for n in range(NCOL):
            if n % 2 == 0:
                @pl.when(z < STAGES - 1)
                def _():
                    hop(n // 2, i, False).wait_recv()

            @pl.when(z == STAGES - 1)
            def _():
                uz[1, n, rows, 0:CH] = sent[1, rows, col(n)]

            acc = acc + nn(uz[1, n, rows, 0:CH], wut[1, col(n), :])

        def finish(part, acc):
            n = 2 * MB + 2 * i + part
            red_tx[n, :, 0:RANK] = acc
            red_tx[n, :, RANK:] = jnp.zeros((TOK, 128), F32)
            red_copy(n).start()
            red_copy(n).wait_recv()
            total = acc + red_rx[n, :, 0:RANK]
            v = pre[part, rows, :]
            gate = jax.nn.sigmoid(v)
            d_pre = total * gate * (1.0 + v * (1.0 - gate))
            scale = scl[part, rows, 0:1]
            mean = jnp.sum(d_pre * v, axis=1, keepdims=True) * (1.0 / D)
            back = (d_pre * scale).astype(BF16)
            for j in range(8):
                uz[part, j, rows, CH:] = back
            return back, mean * scale * scale

        back, shrink = finish(1, acc)
        acc = jnp.zeros((TOK, RANK), F32)
        for n in range(NCOL):
            u = (
                uz[1, n, rows, 0:CH].astype(F32) + nn(back, wdt[1, :, col(n)]) * gn[1, :, col(n)]
                - shrink * xz[1, n, rows, 0:CH].astype(F32)
            ).astype(BF16)
            uz[0, n, rows, 0:CH] = u
            acc = acc + nn(u, wut[0, col(n), :])
        back, shrink = finish(0, acc)

        @pl.when(z > 0)
        def _():
            for n in range(NCOL):
                u = (
                    uz[0, n, rows, 0:CH].astype(F32) + nn(back, wdt[0, :, col(n)]) * gn[0, :, col(n)]
                    - shrink * xz[0, n, rows, 0:CH].astype(F32)
                )
                bout[n, rows, :] = u.astype(BF16)
                if n % 2 == 1:
                    hop(n // 2, i, False).start()

        return carry

    def back_batch(b, carry):
        lax.fori_loop(b * (BATCH // TOK), (b + 1) * (BATCH // TOK), backward, 0)
        rows_start(1, b)
        return carry

    lax.fori_loop(0, NBATCH, back_batch, 0)

    @pl.when(z == STAGES - 1)
    def _():
        early()

    gd_out[...] = jnp.zeros_like(gd_out)
    gu_out[...] = jnp.zeros_like(gu_out)

    def total(b, carry):
        rows_wait(0, b)
        rows_wait(1, b)
        at = pl.ds(pl.multiple_of(16 * BATCH * b, 16 * BATCH), 16 * BATCH)
        gd_out[...] += tn(gxz[at, 0:CH], guz[at, CH:])
        gu_out[...] += tn(gxz[at, CH:], guz[at, 0:CH])
        return carry

    lax.fori_loop(0, NBATCH, total, 0)

    def all_rows_sent(b, carry):
        rows_sent(0, b)
        rows_sent(1, b)
        return carry

    lax.fori_loop(0, NBATCH, all_rows_sent, 0)
    weight_sent()
    gain_far.wait_send()

    @pl.when(z == 0)
    def _():
        end_sent(0)

    @pl.when(z == STAGES - 1)
    def _():
        end_sent(1)

    for k in range(4):
        table_sent(0, k)
        table_sent(1, k)

    def rest(i, carry):
        for n in range(NCOL // 2):
            @pl.when(z < STAGES - 1)
            def _():
                hop(n, i, True).wait_send()

            @pl.when(z > 0)
            def _():
                hop(n, i, False).wait_send()

        for k in range(4):
            red_copy(4 * i + k).wait_send()
        return carry

    lax.fori_loop(0, MB, rest, 0)


def shards(tokens, cotangent, sample_ids, sent_before, received_before, norm_gain, down_proj, up_proj):
    e = lax.axis_index("dp")
    gain = lax.dynamic_slice(norm_gain[0], (e * CH,), (CH,))[:, None]
    any_ = pl.BlockSpec(memory_space=pl.ANY)
    vmem = pl.BlockSpec(memory_space=pltpu.VMEM)
    dma = pltpu.SemaphoreType.DMA
    rows = MB * TOK
    grad_down, grad_up = pl.pallas_call(
        kernel,
        out_shape=(jax.ShapeDtypeStruct((CH, RANK), F32), jax.ShapeDtypeStruct((RANK, CH), F32)),
        in_specs=[pl.BlockSpec(memory_space=pltpu.SMEM)] + [any_] * 7,
        out_specs=(vmem, vmem),
        scratch_shapes=[
            pltpu.VMEM((MB, TOK, D), BF16),
            pltpu.VMEM((4, TOK, D), BF16),
            pltpu.VMEM((2, 1, HALF), F32),
            pltpu.VMEM((2, rows, HALF), BF16),
            pltpu.VMEM((2, rows, HALF), BF16),
            pltpu.VMEM((2, HALF, RANK), BF16),
            pltpu.VMEM((2, RANK, HALF), BF16),
            pltpu.VMEM((2, RANK, HALF), BF16),
            pltpu.VMEM((2, HALF, RANK), BF16),
            pltpu.VMEM((rows, HALF), BF16),
            pltpu.VMEM((2, 8, rows, PACK), BF16),
            pltpu.VMEM((2, 8, rows, PACK), BF16),
            pltpu.VMEM((TOK, HALF), F32),
            pltpu.VMEM((rows, HALF), BF16),
            pltpu.VMEM((8, rows, CH), BF16),
            pltpu.VMEM((4 * MB, TOK, RANK + 128), F32),
            pltpu.VMEM((4 * MB, TOK, RANK + 128), F32),
            pltpu.VMEM((2, rows, RANK), F32),
            pltpu.VMEM((2, rows, 128), F32),
            pltpu.VMEM((16 * rows, PACK), BF16),
            pltpu.VMEM((16 * rows, PACK), BF16),
            dma, dma((4,)),
            dma, dma((2,)),
            dma((2, 4, 4)), dma((2, 2, MB)),
            dma((4,)), dma((2, 2)), dma((2, 4)), dma((2, 4)), dma((2, 2)), dma((2, 2)),
            dma((4,)), dma((8,)), dma((4, 4)), dma((2, 4)), dma((2, 4)), dma((4, 2)),
            dma((MB, NCOL // 2)), dma((MB, NCOL // 2)),
            dma((MB, NCOL // 2)), dma((MB, NCOL // 2)),
            dma((4 * MB,)), dma((4 * MB,)),
            dma((2, NBATCH, 2, 8)), dma((2, NBATCH, 16)),
        ],
        compiler_params=pltpu.CompilerParams(
            collective_id=0, has_side_effects=True, vmem_limit_bytes=56 * 1024 * 1024
        ),
    )(sample_ids, received_before[0], sent_before[0], tokens, cotangent, norm_gain, down_proj[0], up_proj[0])
    return ((grad_down * gain)[None], grad_up[None])


def solution(mesh):
    placed = (
        P(None, "dp", None),
        P(None, "dp", None),
        P("dp", None),
        P("section", "dp", None, None),
        P("section", "dp", None, None),
        P("section", None),
        P("section", "dp", None),
        P("section", None, "dp"),
    )
    return jax.shard_map(
        shards,
        mesh=mesh,
        in_specs=placed,
        out_specs=(P("section", "dp", None), P("section", None, "dp")),
        check_vma=False,
    )
```

```python
import functools

import jax
import jax.numpy as jnp
from jax import lax
from jax.experimental import pallas as pl
from jax.experimental.pallas import tpu as pltpu
from jax.sharding import PartitionSpec as P

MESH = pl.DeviceIdType.MESH
F32, BF16 = jnp.float32, jnp.bfloat16
EPS = 1e-05
D = 8192
HALF = 4096
RANK = 256
TOK = 16
MB = 8
CH = 512
COLS = 512
NCOL = HALF // COLS
STAGES = 8
BATCH = 2 * TOK
NBATCH = MB * TOK // BATCH
PACK = CH + RANK


def tn(a, b):
    return lax.dot_general(a, b, (((0,), (0,)), ((), ())), preferred_element_type=F32)


def nn(a, b):
    return jnp.dot(a, b, preferred_element_type=F32)


def lanes(v):
    total = v[:, 0:128]
    for k in range(128, v.shape[1], 128):
        total = total + v[:, k : k + 128]
    return total


def kernel(
    ids, rec_in, sent_in, tok_in, cot_in, gain_in, down_in, up_in, gd_out, gu_out,
    raw, perm, gn, rec, sent, wd, wu, wdt, wut, xin, xz, uz, xf, fout, bout, red_tx, red_rx,
    bred_tx, bred_rx, gt_tx, gt_rx, zed_tx, zed_rx, gt, zed, pre, scl, gxz, guz,
    c_raw, s_tok, s_gn, r_gn, s_tab, r_tab, s_w, r_w, s_x, r_x, s_xr, r_xr,
    s_u, r_u, s_v, r_v, s_vr, r_vr,
    s_hf, r_hf, s_hb, r_hb, s_red, r_red, s_br, r_br, s_one, r_one, s_g, r_g,
):
    s = lax.axis_index("section")
    e = lax.axis_index("dp")
    h, z = lax.rem(s, 2), lax.div(s, 2)
    c, q = lax.rem(e, 2), lax.div(e, 2)
    chip = h * 8 + q
    owner_core = lax.div(e, 8)
    local = c == owner_core
    other = (s, e + 1 - 2 * c)

    raw_tok = pltpu.make_async_copy(tok_in, raw, c_raw)
    raw_cot = pltpu.make_async_copy(cot_in, raw, c_raw)

    @pl.when(z == 0)
    def _():
        raw_tok.start()

    @pl.when(z == STAGES - 1)
    def _():
        raw_cot.start()

    barrier = pltpu.get_barrier_semaphore()

    def greet(t, carry):
        place = lax.rem(h * 16 + e + t, 32)
        pl.semaphore_signal(
            barrier, inc=1, device_id=(2 * z + lax.div(place, 16), lax.rem(place, 16)), device_id_type=MESH
        )
        return carry

    lax.fori_loop(1, 32, greet, 0)

    @pl.when(z > 0)
    def _():
        pl.semaphore_signal(barrier, inc=1, device_id=(s - 2, e), device_id_type=MESH)

    @pl.when(z < STAGES - 1)
    def _():
        pl.semaphore_signal(barrier, inc=1, device_id=(s + 2, e), device_id_type=MESH)

    neighbours = jnp.where(z > 0, 1, 0) + jnp.where(z < STAGES - 1, 1, 0)
    pl.semaphore_wait(barrier, 31 + neighbours)

    def table_copy(which, k, t):
        src = (rec_in, sent_in)[which]
        dst = (rec, sent)[which]
        h2, c2 = lax.rem(h + t // 2, 2), lax.rem(c + t, 2)
        row = pl.multiple_of((2 * k + c) * TOK, TOK)
        return dict(
            src_ref=src.at[4 * h2 + k, :, pl.ds(pl.multiple_of(c2 * HALF, HALF), HALF)],
            dst_ref=dst.at[h, pl.ds(row, TOK), :],
        ), s_tab.at[which, k, t], r_tab.at[which, h, 2 * k + c], (2 * z + h2, 2 * q + c2)

    def table_used(which):
        return s != (0, 2 * STAGES - 1)[which]

    def table_start(which, k):
        @pl.when(table_used(which))
        def _():
            for t in range(4):
                refs, ssem, rsem, dev = table_copy(which, k, t)
                if t == 0:
                    pltpu.make_async_copy(refs["src_ref"], refs["dst_ref"], rsem).start()
                else:
                    pltpu.make_async_remote_copy(
                        **refs, send_sem=ssem, recv_sem=rsem, device_id=dev, device_id_type=MESH
                    ).start()

    def table_sent(which, k):
        @pl.when(table_used(which))
        def _():
            for t in range(1, 4):
                refs, ssem, rsem, dev = table_copy(which, k, t)
                pltpu.make_async_remote_copy(
                    **refs, send_sem=ssem, recv_sem=rsem, device_id=dev, device_id_type=MESH
                ).wait_send()

    def end_copies(which, k):
        dst, part = ((rec, 0), (sent, 1))[which]
        place = dst.at[part, pl.ds(pl.multiple_of((2 * k + c) * TOK, TOK), TOK), :]
        rsem = r_tab.at[which, part, 2 * k + c]
        mine = perm.at[k, :, pl.ds(pl.multiple_of(c * HALF, HALF), HALF)]
        return mine, place, rsem

    def end_far(which, k):
        theirs = perm.at[k, :, pl.ds(pl.multiple_of((1 - c) * HALF, HALF), HALF)]
        place, rsem = end_copies(which, k)[1:]
        return pltpu.make_async_remote_copy(
            src_ref=theirs, dst_ref=place, send_sem=s_tok.at[k], recv_sem=rsem, device_id=other, device_id_type=MESH
        )

    def end_start(which):
        (raw_tok, raw_cot)[which].wait()
        for k in range(4):
            at = jnp.int32(0)
            for m in range(1, MB):
                at = jnp.where(ids[0, m] == 4 * h + k, m, at)
            at = jnp.clip(at, 0, MB - 1)

            def move(n, carry, at=at, k=k):
                cols = pl.ds(pl.multiple_of(n * 1024, 1024), 1024)
                perm[k, :, cols] = raw[at, :, cols]
                return carry

            lax.fori_loop(0, D // 1024, move, 0)
            end_far(which, k).start()
            pltpu.make_async_copy(*end_copies(which, k)).start()

    def end_sent(which):
        for k in range(4):
            end_far(which, k).wait_send()

    def table_wait(which, part, i):
        place = (rec, sent)[which].at[part, pl.ds(pl.multiple_of(i * TOK, TOK), TOK), :]
        pltpu.make_async_copy(place, place, r_tab.at[which, part, i]).wait()

    slot = lax.rem(e, 8)
    spot = pl.ds(pl.multiple_of(slot * CH, CH), CH)
    col_x = lax.rem(q, 4)
    row_y = 2 * h + owner_core

    def device(x, y, core):
        return (2 * z + lax.div(y, 2), 8 * lax.rem(y, 2) + 2 * x + core)

    def wide(x):
        return pl.ds(pl.multiple_of(x * 2 * CH, 2 * CH), 2 * CH)

    def away(t):
        return lax.rem(col_x + t, 4)

    def w_remote(t):
        return pltpu.make_async_remote_copy(
            src_ref=down_in, dst_ref=wd.at[h, spot, :], send_sem=s_w.at[t], recv_sem=r_w.at[h, c],
            device_id=device(col_x, lax.rem(row_y + t, 4), owner_core), device_id_type=MESH,
        )

    def u_remote(t):
        return pltpu.make_async_remote_copy(
            src_ref=up_in, dst_ref=wu.at[h, :, spot], send_sem=s_u.at[t], recv_sem=r_u.at[slot],
            device_id=device(away(t), row_y, owner_core), device_id_type=MESH,
        )

    def first_start():
        @pl.when(local)
        def _():
            pltpu.make_async_copy(down_in, wd.at[h, spot, :], r_w.at[h, c]).start()

        @pl.when(jnp.logical_not(local))
        def _():
            w_remote(0).start()

        for t in (1, 3, 2):
            w_remote(t).start()

        @pl.when(local)
        def _():
            pltpu.make_async_copy(up_in, wu.at[h, :, spot], r_u.at[slot]).start()

        @pl.when(jnp.logical_not(local))
        def _():
            u_remote(0).start()

        for t in (1, 3, 2):
            u_remote(t).start()

    def first_sent():
        @pl.when(jnp.logical_not(local))
        def _():
            w_remote(0).wait_send()
            u_remote(0).wait_send()

        for t in range(1, 4):
            w_remote(t).wait_send()
            u_remote(t).wait_send()

    def w_block(part, t):
        place = wd.at[part, wide(col_x), :]
        return pltpu.make_async_remote_copy(
            src_ref=place, dst_ref=place, send_sem=s_x.at[part, t], recv_sem=r_x.at[part, col_x],
            device_id=(s, e - 2 * col_x + 2 * away(t)), device_id_type=MESH,
        )

    def w_start(part):
        for j in range(2):
            place = wd.at[part, pl.ds(pl.multiple_of((2 * col_x + j) * CH, CH), CH), :]
            pltpu.make_async_copy(place, place, r_w.at[part, j]).wait()
        for t in (1, 3):
            w_block(part, t).start()

    def w_half(part, x, half):
        return wd.at[part, pl.ds(pl.multiple_of((2 * x + half) * CH, CH), CH), :]

    def w_relay(part, half):
        place = w_half(part, away((3, 1)[half]), half)
        return pltpu.make_async_remote_copy(
            src_ref=place, dst_ref=place, send_sem=s_xr.at[part, half], recv_sem=r_xr.at[part, half],
            device_id=(s, e - 2 * col_x + 2 * away((1, 3)[half])), device_id_type=MESH,
        )

    def w_forward(part):
        for half in range(2):
            x = away((3, 1)[half])
            place = wd.at[part, wide(x), :]
            pltpu.make_async_copy(place, place, r_x.at[part, x]).wait()
            w_relay(part, half).start()

    def u_block(n, t):
        place = wu.at[h, :, wide(away(n))]
        return pltpu.make_async_remote_copy(
            src_ref=place, dst_ref=place, send_sem=s_v.at[n, t], recv_sem=r_v.at[h, away(n)],
            device_id=device(col_x, lax.rem(row_y + t, 4), c), device_id_type=MESH,
        )

    def u_start(n):
        @pl.when(local)
        def _():
            for j in range(2):
                at = 2 * away(n) + j
                place = wu.at[h, :, pl.ds(pl.multiple_of(at * CH, CH), CH)]
                pltpu.make_async_copy(place, place, r_u.at[at]).wait()
            for t in (1, 3):
                u_block(n, t).start()

    y_me = 2 * h + lax.div(e, 8)

    def u_half(part, n, half):
        return wu.at[part, pl.ds(pl.multiple_of(half * (RANK // 2), RANK // 2), RANK // 2), wide(away(n))]

    def u_relay(part, n):
        half = jnp.where(lax.rem(y_me - 2 * part - c + 4, 4) == 1, 0, 1)
        place = u_half(part, n, half)
        return pltpu.make_async_remote_copy(
            src_ref=place, dst_ref=place, send_sem=s_vr.at[part, n], recv_sem=r_vr.at[n, half],
            device_id=device(col_x, lax.rem(y_me + 1 + 2 * half, 4), c), device_id_type=MESH,
        )

    def u_forward(n):
        @pl.when(jnp.logical_not(local))
        def _():
            for part in range(2):
                place = wu.at[part, :, wide(away(n))]
                pltpu.make_async_copy(place, place, r_v.at[part, away(n)]).wait()
                u_relay(part, n).start()

    def weight_wait(kind, part):
        if kind == 0:
            for half in range(2):
                place = w_half(part, away(2), half)
                pltpu.make_async_copy(place, place, r_xr.at[part, half]).wait()
        else:
            @pl.when(jnp.logical_and(local, h != part))
            def _():
                for n in range(4):
                    for half in range(2):
                        place = u_half(part, n, half)
                        pltpu.make_async_copy(place, place, r_vr.at[n, half]).wait()

    def weight_sent():
        first_sent()
        for part in range(2):
            for t in (1, 3):
                w_block(part, t).wait_send()
            for half in range(2):
                w_relay(part, half).wait_send()

        @pl.when(local)
        def _():
            for n in range(4):
                for t in (1, 3):
                    u_block(n, t).wait_send()

        @pl.when(jnp.logical_not(local))
        def _():
            for n in range(4):
                for part in range(2):
                    u_relay(part, n).wait_send()

    gain_part = gain_in.at[:, pl.ds(pl.multiple_of(c * HALF, HALF), HALF)]
    gain_near = pltpu.make_async_copy(gain_part, gn.at[h], r_gn.at[h])
    gain_far = pltpu.make_async_remote_copy(
        src_ref=gain_part, dst_ref=gn.at[h], send_sem=s_gn, recv_sem=r_gn.at[h],
        device_id=(s + 1 - 2 * h, e), device_id_type=MESH,
    )

    first_start()
    gain_near.start()
    gain_far.start()
    table_start(0, 0)
    table_start(1, 0)

    @pl.when(z == 0)
    def _():
        end_start(0)

    @pl.when(z == STAGES - 1)
    def _():
        end_start(1)

    w_start(0)
    u_start(0)
    w_start(1)
    for n in (1, 3, 2):
        u_start(n)
    w_forward(0)
    u_forward(0)
    w_forward(1)
    u_forward(1)
    u_forward(3)
    table_start(0, 1)
    table_start(1, 1)
    u_forward(2)
    for part in range(2):
        pltpu.make_async_copy(gn.at[part], gn.at[part], r_gn.at[part]).wait()

    def red_copy(n):
        return pltpu.make_async_remote_copy(
            src_ref=red_tx.at[n], dst_ref=red_rx.at[n], send_sem=s_red.at[n], recv_sem=r_red.at[n],
            device_id=other, device_id_type=MESH,
        )

    def bred_copy(i):
        return pltpu.make_async_remote_copy(
            src_ref=bred_tx.at[i], dst_ref=bred_rx.at[i], send_sem=s_br.at[i], recv_sem=r_br.at[i],
            device_id=other, device_id_type=MESH,
        )

    def one_copy(n):
        src, dst = ((gt_tx, gt_rx), (zed_tx, zed_rx))[n]
        return pltpu.make_async_remote_copy(
            src_ref=src, dst_ref=dst, send_sem=s_one.at[n], recv_sem=r_one.at[n], device_id=other, device_id_type=MESH
        )

    def col(n):
        return slice(n * COLS, (n + 1) * COLS)

    def hop(n, i, ahead):
        rows = pl.ds(pl.multiple_of(i * TOK, TOK), TOK)
        if ahead:
            wide_col = slice(2 * n * COLS, 2 * (n + 1) * COLS)
            src, dst, ss, rs, dev = fout.at[rows, wide_col], xin.at[rows, wide_col], s_hf, r_hf, (s + 2, e)
        else:
            two = pl.ds(2 * n, 2)
            src, dst, ss, rs, dev = bout.at[two, rows, :], uz.at[1, two, rows, pl.ds(0, CH)], s_hb, r_hb, (s - 2, e)
        return pltpu.make_async_remote_copy(
            src_ref=src, dst_ref=dst, send_sem=ss.at[i, n], recv_sem=rs.at[i, n], device_id=dev, device_id_type=MESH
        )

    def rows_copy(kind, b, part, j):
        src = (xz, uz)[kind].at[part, j, pl.ds(pl.multiple_of(b * BATCH, BATCH), BATCH), :]
        return src, landing(kind, b, chip), s_g.at[kind, b, part, j], r_g.at[kind, b, chip], (2 * z + part, 8 * c + j)

    def landing(kind, b, source):
        at = pl.ds(pl.multiple_of((16 * b + source) * BATCH, BATCH), BATCH)
        return (gxz, guz)[kind].at[at, :]

    def rows_each(kind, b, own, far):
        def one(t, carry):
            place = lax.rem(chip + t, 16)
            part, j = lax.div(place, 8), lax.rem(place, 8)
            src, dst, ssem, rsem, dev = rows_copy(kind, b, part, j)
            mine = jnp.logical_and(h == part, 8 * c + j == e)
            if own:
                @pl.when(mine)
                def _():
                    pltpu.make_async_copy(src, dst, rsem).start()

            @pl.when(jnp.logical_not(mine))
            def _():
                far(
                    pltpu.make_async_remote_copy(
                        src_ref=src, dst_ref=dst, send_sem=ssem, recv_sem=rsem, device_id=dev, device_id_type=MESH
                    )
                )

            return carry

        lax.fori_loop(0, 16, one, 0)

    def rows_start(kind, b):
        rows_each(kind, b, True, lambda copy: copy.start())

    def rows_sent(kind, b):
        rows_each(kind, b, False, lambda copy: copy.wait_send())

    def rows_wait(kind, b):
        def one(t, carry):
            place = landing(kind, b, t)
            pltpu.make_async_copy(place, place, r_g.at[kind, b, t]).wait()
            return carry

        lax.fori_loop(0, 16, one, 0)

    def turn():
        for part in range(2):
            def one(j, carry, part=part):
                at = pl.ds(pl.multiple_of(j * CH, CH), CH)
                wdt[part, :, at] = wd[part, at, :].T
                wut[part, at, :] = wu[part, :, at].T
                return carry

            lax.fori_loop(0, HALF // CH, one, 0)

        gt_tx[...] = jnp.zeros_like(gt_tx)

        def product(j, carry):
            at = pl.ds(pl.multiple_of(j * CH, CH), CH)
            gt_tx[...] += nn((wdt[1, :, at].astype(F32) * gn[1, :, at]).astype(BF16), wut[0, at, :])
            return carry

        lax.fori_loop(0, HALF // CH, product, 0)
        one_copy(0).start()
        one_copy(0).wait_recv()
        gt[...] = (gt_tx[...] + gt_rx[...]).astype(BF16)

    late = z >= STAGES // 2

    @pl.when(late)
    def _():
        for kind in range(2):
            for part in range(2):
                weight_wait(kind, part)
        turn()

    def forward(i, carry):
        rows = pl.ds(pl.multiple_of(i * TOK, TOK), TOK)
        fresh = jnp.logical_and(i == 0, jnp.logical_not(late))
        table_wait(0, 0, i)

        @pl.when(i == 0)
        def _():
            table_start(0, 2)
            table_start(1, 2)

        @pl.when(i == 2)
        def _():
            table_start(0, 3)
            table_start(1, 3)


        @pl.when(fresh)
        def _():
            weight_wait(0, 0)

        acc = jnp.zeros((TOK, RANK), F32)
        sq = jnp.zeros((TOK, 128), F32)
        for n in range(NCOL):
            @pl.when(z > 0)
            def _():
                if n % 2 == 0:
                    hop(n // 2, i, True).wait_recv()
                xf[:, col(n)] = rec[0, rows, col(n)].astype(F32) + xin[rows, col(n)].astype(F32)

            @pl.when(z == 0)
            def _():
                xf[:, col(n)] = rec[0, rows, col(n)].astype(F32)

            x = xf[:, col(n)]
            xz[0, n, rows, 0:CH] = x.astype(BF16)
            sq = sq + lanes(x * x)
            acc = acc + nn((x * gn[0, :, col(n)]).astype(BF16), wd[0, col(n), :])

        def finish(part, acc, sq):
            n = 2 * i + part
            red_tx[n, :, 0:RANK] = acc
            red_tx[n, :, RANK:] = sq
            red_copy(n).start()
            red_copy(n).wait_recv()
            total = acc + red_rx[n, :, 0:RANK]
            square = jnp.sum(sq + red_rx[n, :, RANK:], axis=1, keepdims=True)
            scale = lax.rsqrt(square * (1.0 / D) + EPS)
            v = total * scale
            pre[part, rows, :] = v
            scl[part, rows, :] = jnp.broadcast_to(scale, (TOK, 128))
            a = (v * jax.nn.sigmoid(v)).astype(BF16)
            for j in range(8):
                xz[part, j, rows, CH:] = a
            return a

        a = finish(0, acc, sq)

        @pl.when(fresh)
        def _():
            weight_wait(1, 0)
            weight_wait(0, 1)

        table_wait(0, 1, i)
        table_wait(1, 0, i)
        acc = jnp.zeros((TOK, RANK), F32)
        sq = jnp.zeros((TOK, 128), F32)
        for n in range(NCOL):
            x = (
                xf[:, col(n)] + nn(a, wu[0, :, col(n)])
                + (rec[1, rows, col(n)].astype(F32) - sent[0, rows, col(n)].astype(F32))
            )
            xf[:, col(n)] = x
            xz[1, n, rows, 0:CH] = x.astype(BF16)
            sq = sq + lanes(x * x)
            acc = acc + nn((x * gn[1, :, col(n)]).astype(BF16), wd[1, col(n), :])
        a = finish(1, acc, sq)

        @pl.when(fresh)
        def _():
            weight_wait(1, 1)

        table_wait(1, 1, i)

        @pl.when(z < STAGES - 1)
        def _():
            for n in range(NCOL):
                x = xf[:, col(n)] + nn(a, wu[1, :, col(n)]) - sent[1, rows, col(n)].astype(F32)
                fout[rows, col(n)] = x.astype(BF16)
                if n % 2 == 1:
                    hop(n // 2, i, True).start()

        return carry

    lax.fori_loop(0, MB, forward, 0)

    @pl.when(jnp.logical_not(late))
    def _():
        turn()

    zed_tx[...] = jnp.zeros_like(zed_tx)
    for n in range(NCOL):
        zed_tx[...] += nn(xz[1, n, :, 0:CH], wut[0, col(n), :])
    one_copy(1).start()
    one_copy(1).wait_recv()
    zed[...] = zed_tx[...] + zed_rx[...]

    def early():
        def one(b, carry):
            rows_start(0, b)
            return carry

        lax.fori_loop(0, NBATCH, one, 0)

    @pl.when(z < STAGES - 1)
    def _():
        early()

    def backward(i, carry):
        rows = pl.ds(pl.multiple_of(i * TOK, TOK), TOK)

        def slope(part):
            v = pre[part, rows, :]
            gate = jax.nn.sigmoid(v)
            return v, gate * (1.0 + v * (1.0 - gate)), scl[part, rows, 0:1]

        v1, slope1, scale1 = slope(1)
        v0, slope0, scale0 = slope(0)
        acc1 = jnp.zeros((TOK, RANK), F32)
        acc0 = jnp.zeros((TOK, RANK), F32)
        for n in range(NCOL):
            if n % 2 == 0:
                @pl.when(z < STAGES - 1)
                def _():
                    hop(n // 2, i, False).wait_recv()

            @pl.when(z == STAGES - 1)
            def _():
                uz[1, n, rows, 0:CH] = sent[1, rows, col(n)]

            u = uz[1, n, rows, 0:CH]
            acc1 = acc1 + nn(u, wut[1, col(n), :])
            acc0 = acc0 + nn(u, wut[0, col(n), :])
        bred_tx[i, :, 0:RANK] = acc1
        bred_tx[i, :, RANK:] = acc0
        bred_copy(i).start()
        bred_copy(i).wait_recv()

        def finish(d_pre, v, scale):
            mean = jnp.sum(d_pre * v, axis=1, keepdims=True) * (1.0 / D)
            return (d_pre * scale).astype(BF16), mean * scale * scale

        back1, shrink1 = finish((acc1 + bred_rx[i, :, 0:RANK]) * slope1, v1, scale1)
        d_act = acc0 + bred_rx[i, :, RANK:] + nn(back1, gt[...]) - shrink1 * zed[rows, :]
        back0, shrink0 = finish(d_act * slope0, v0, scale0)
        for n in range(NCOL):
            u = (
                uz[1, n, rows, 0:CH].astype(F32) + nn(back1, wdt[1, :, col(n)]) * gn[1, :, col(n)]
                - shrink1 * xz[1, n, rows, 0:CH].astype(F32)
            ).astype(BF16)
            uz[0, n, rows, 0:CH] = u
            uz[1, n, rows, CH:] = back1
            uz[0, n, rows, CH:] = back0
            u = (
                u.astype(F32) + nn(back0, wdt[0, :, col(n)]) * gn[0, :, col(n)]
                - shrink0 * xz[0, n, rows, 0:CH].astype(F32)
            )
            bout[n, rows, :] = u.astype(BF16)
            if n % 2 == 1:
                @pl.when(z > 0)
                def _():
                    hop(n // 2, i, False).start()

        return carry

    def back_batch(b, carry):
        lax.fori_loop(b * (BATCH // TOK), (b + 1) * (BATCH // TOK), backward, 0)
        rows_start(1, b)
        return carry

    lax.fori_loop(0, NBATCH, back_batch, 0)

    @pl.when(z == STAGES - 1)
    def _():
        early()

    gd_out[...] = jnp.zeros_like(gd_out)
    gu_out[...] = jnp.zeros_like(gu_out)

    def total(b, carry):
        rows_wait(0, b)
        rows_wait(1, b)
        at = pl.ds(pl.multiple_of(16 * BATCH * b, 16 * BATCH), 16 * BATCH)
        gd_out[...] += tn(gxz[at, 0:CH], guz[at, CH:])
        gu_out[...] += tn(gxz[at, CH:], guz[at, 0:CH])
        return carry

    lax.fori_loop(0, NBATCH, total, 0)

    def all_rows_sent(b, carry):
        rows_sent(0, b)
        rows_sent(1, b)
        return carry

    lax.fori_loop(0, NBATCH, all_rows_sent, 0)
    weight_sent()
    gain_far.wait_send()

    @pl.when(z == 0)
    def _():
        end_sent(0)

    @pl.when(z == STAGES - 1)
    def _():
        end_sent(1)

    for k in range(4):
        table_sent(0, k)
        table_sent(1, k)

    def rest(i, carry):
        for n in range(NCOL // 2):
            @pl.when(z < STAGES - 1)
            def _():
                hop(n, i, True).wait_send()

            @pl.when(z > 0)
            def _():
                hop(n, i, False).wait_send()

        for k in range(2):
            red_copy(2 * i + k).wait_send()
        bred_copy(i).wait_send()
        return carry

    lax.fori_loop(0, MB, rest, 0)
    one_copy(0).wait_send()
    one_copy(1).wait_send()


def shards(tokens, cotangent, sample_ids, sent_before, received_before, norm_gain, down_proj, up_proj):
    e = lax.axis_index("dp")
    gain = lax.dynamic_slice(norm_gain[0], (e * CH,), (CH,))[:, None]
    any_ = pl.BlockSpec(memory_space=pl.ANY)
    vmem = pl.BlockSpec(memory_space=pltpu.VMEM)
    dma = pltpu.SemaphoreType.DMA
    rows = MB * TOK
    grad_down, grad_up = pl.pallas_call(
        kernel,
        out_shape=(jax.ShapeDtypeStruct((CH, RANK), F32), jax.ShapeDtypeStruct((RANK, CH), F32)),
        in_specs=[pl.BlockSpec(memory_space=pltpu.SMEM)] + [any_] * 7,
        out_specs=(vmem, vmem),
        scratch_shapes=[
            pltpu.VMEM((MB, TOK, D), BF16),
            pltpu.VMEM((4, TOK, D), BF16),
            pltpu.VMEM((2, 1, HALF), F32),
            pltpu.VMEM((2, rows, HALF), BF16),
            pltpu.VMEM((2, rows, HALF), BF16),
            pltpu.VMEM((2, HALF, RANK), BF16),
            pltpu.VMEM((2, RANK, HALF), BF16),
            pltpu.VMEM((2, RANK, HALF), BF16),
            pltpu.VMEM((2, HALF, RANK), BF16),
            pltpu.VMEM((rows, HALF), BF16),
            pltpu.VMEM((2, 8, rows, PACK), BF16),
            pltpu.VMEM((2, 8, rows, PACK), BF16),
            pltpu.VMEM((TOK, HALF), F32),
            pltpu.VMEM((rows, HALF), BF16),
            pltpu.VMEM((8, rows, CH), BF16),
            pltpu.VMEM((2 * MB, TOK, RANK + 128), F32),
            pltpu.VMEM((2 * MB, TOK, RANK + 128), F32),
            pltpu.VMEM((MB, TOK, 2 * RANK), F32),
            pltpu.VMEM((MB, TOK, 2 * RANK), F32),
            pltpu.VMEM((RANK, RANK), F32),
            pltpu.VMEM((RANK, RANK), F32),
            pltpu.VMEM((rows, RANK), F32),
            pltpu.VMEM((rows, RANK), F32),
            pltpu.VMEM((RANK, RANK), BF16),
            pltpu.VMEM((rows, RANK), F32),
            pltpu.VMEM((2, rows, RANK), F32),
            pltpu.VMEM((2, rows, 128), F32),
            pltpu.VMEM((16 * rows, PACK), BF16),
            pltpu.VMEM((16 * rows, PACK), BF16),
            dma, dma((4,)),
            dma, dma((2,)),
            dma((2, 4, 4)), dma((2, 2, MB)),
            dma((4,)), dma((2, 2)), dma((2, 4)), dma((2, 4)), dma((2, 2)), dma((2, 2)),
            dma((4,)), dma((8,)), dma((4, 4)), dma((2, 4)), dma((2, 4)), dma((4, 2)),
            dma((MB, NCOL // 2)), dma((MB, NCOL // 2)),
            dma((MB, NCOL // 2)), dma((MB, NCOL // 2)),
            dma((2 * MB,)), dma((2 * MB,)), dma((MB,)), dma((MB,)), dma((2,)), dma((2,)),
            dma((2, NBATCH, 2, 8)), dma((2, NBATCH, 16)),
        ],
        compiler_params=pltpu.CompilerParams(
            collective_id=0, has_side_effects=True, vmem_limit_bytes=56 * 1024 * 1024
        ),
    )(sample_ids, received_before[0], sent_before[0], tokens, cotangent, norm_gain, down_proj[0], up_proj[0])
    return ((grad_down * gain)[None], grad_up[None])


def solution(mesh):
    placed = (
        P(None, "dp", None),
        P(None, "dp", None),
        P("dp", None),
        P("section", "dp", None, None),
        P("section", "dp", None, None),
        P("section", None),
        P("section", "dp", None),
        P("section", None, "dp"),
    )
    return jax.shard_map(
        shards,
        mesh=mesh,
        in_specs=placed,
        out_specs=(P("section", "dp", None), P("section", None, "dp")),
        check_vma=False,
    )
```

```python
import functools

import jax
import jax.numpy as jnp
from jax import lax
from jax.experimental import pallas as pl
from jax.experimental.pallas import tpu as pltpu
from jax.sharding import PartitionSpec as P

MESH = pl.DeviceIdType.MESH
F32, BF16 = jnp.float32, jnp.bfloat16
EPS = 1e-05
D = 8192
HALF = 4096
RANK = 256
TOK = 16
MB = 8
CH = 512
COLS = 512
NCOL = HALF // COLS
STAGES = 8
BATCH = 2 * TOK
NBATCH = MB * TOK // BATCH
PACK = CH + RANK
LOW = 128


def tn(a, b):
    return lax.dot_general(a, b, (((0,), (0,)), ((), ())), preferred_element_type=F32)


def nn(a, b):
    return jnp.dot(a, b, preferred_element_type=F32)


def lanes(v):
    total = v[:, 0:128]
    for k in range(128, v.shape[1], 128):
        total = total + v[:, k : k + 128]
    return total


def kernel(
    ids, rec_in, sent_in, tok_in, cot_in, gain_in, down_in, up_in, gd_out, gu_out,
    raw, perm, gn, rec, sent, wd, wu, wdt, wut, xin, xz, uz, xf, fout, bout, red_tx, red_rx,
    bred_tx, bred_rx, gt_tx, gt_rx, zed_tx, zed_rx, gt, zed, pre, scl, gxz, guz,
    c_raw, s_tok, s_gn, r_gn, s_tab, r_tab, s_w, r_w, s_x, r_x, s_xr, r_xr,
    s_u, r_u, s_v, r_v, s_vr, r_vr,
    s_hf, r_hf, s_hb, r_hb, s_red, r_red, s_br, r_br, s_one, r_one, s_g, r_g,
):
    s = lax.axis_index("section")
    e = lax.axis_index("dp")
    h, z = lax.rem(s, 2), lax.div(s, 2)
    c, q = lax.rem(e, 2), lax.div(e, 2)
    chip = h * 8 + q
    owner_core = lax.div(e, 8)
    local = c == owner_core
    other = (s, e + 1 - 2 * c)

    raw_tok = pltpu.make_async_copy(tok_in, raw, c_raw)
    raw_cot = pltpu.make_async_copy(cot_in, raw, c_raw)

    @pl.when(z == 0)
    def _():
        raw_tok.start()

    @pl.when(z == STAGES - 1)
    def _():
        raw_cot.start()

    barrier = pltpu.get_barrier_semaphore()

    def greet(t, carry):
        place = lax.rem(h * 16 + e + t, 32)
        pl.semaphore_signal(
            barrier, inc=1, device_id=(2 * z + lax.div(place, 16), lax.rem(place, 16)), device_id_type=MESH
        )
        return carry

    lax.fori_loop(1, 32, greet, 0)

    @pl.when(z > 0)
    def _():
        pl.semaphore_signal(barrier, inc=1, device_id=(s - 2, e), device_id_type=MESH)

    @pl.when(z < STAGES - 1)
    def _():
        pl.semaphore_signal(barrier, inc=1, device_id=(s + 2, e), device_id_type=MESH)

    neighbours = jnp.where(z > 0, 1, 0) + jnp.where(z < STAGES - 1, 1, 0)
    pl.semaphore_wait(barrier, 31 + neighbours)

    def table_copy(which, k, t):
        src = (rec_in, sent_in)[which]
        dst = (rec, sent)[which]
        h2, c2 = lax.rem(h + t // 2, 2), lax.rem(c + t, 2)
        row = pl.multiple_of((2 * k + c) * TOK, TOK)
        return dict(
            src_ref=src.at[4 * h2 + k, :, pl.ds(pl.multiple_of(c2 * HALF, HALF), HALF)],
            dst_ref=dst.at[h, pl.ds(row, TOK), :],
        ), s_tab.at[which, k, t], r_tab.at[which, h, 2 * k + c], (2 * z + h2, 2 * q + c2)

    def table_used(which):
        return s != (0, 2 * STAGES - 1)[which]

    def table_start(which, k):
        @pl.when(table_used(which))
        def _():
            for t in range(4):
                refs, ssem, rsem, dev = table_copy(which, k, t)
                if t == 0:
                    pltpu.make_async_copy(refs["src_ref"], refs["dst_ref"], rsem).start()
                else:
                    pltpu.make_async_remote_copy(
                        **refs, send_sem=ssem, recv_sem=rsem, device_id=dev, device_id_type=MESH
                    ).start()

    def table_sent(which, k):
        @pl.when(table_used(which))
        def _():
            for t in range(1, 4):
                refs, ssem, rsem, dev = table_copy(which, k, t)
                pltpu.make_async_remote_copy(
                    **refs, send_sem=ssem, recv_sem=rsem, device_id=dev, device_id_type=MESH
                ).wait_send()

    def end_copies(which, k):
        dst, part = ((rec, 0), (sent, 1))[which]
        place = dst.at[part, pl.ds(pl.multiple_of((2 * k + c) * TOK, TOK), TOK), :]
        rsem = r_tab.at[which, part, 2 * k + c]
        mine = perm.at[k, :, pl.ds(pl.multiple_of(c * HALF, HALF), HALF)]
        return mine, place, rsem

    def end_far(which, k):
        theirs = perm.at[k, :, pl.ds(pl.multiple_of((1 - c) * HALF, HALF), HALF)]
        place, rsem = end_copies(which, k)[1:]
        return pltpu.make_async_remote_copy(
            src_ref=theirs, dst_ref=place, send_sem=s_tok.at[k], recv_sem=rsem, device_id=other, device_id_type=MESH
        )

    def end_start(which):
        (raw_tok, raw_cot)[which].wait()
        for k in range(4):
            at = jnp.int32(0)
            for m in range(1, MB):
                at = jnp.where(ids[0, m] == 4 * h + k, m, at)
            at = jnp.clip(at, 0, MB - 1)

            def move(n, carry, at=at, k=k):
                cols = pl.ds(pl.multiple_of(n * 1024, 1024), 1024)
                perm[k, :, cols] = raw[at, :, cols]
                return carry

            lax.fori_loop(0, D // 1024, move, 0)
            end_far(which, k).start()
            pltpu.make_async_copy(*end_copies(which, k)).start()

    def end_sent(which):
        for k in range(4):
            end_far(which, k).wait_send()

    def table_wait(which, part, i):
        place = (rec, sent)[which].at[part, pl.ds(pl.multiple_of(i * TOK, TOK), TOK), :]
        pltpu.make_async_copy(place, place, r_tab.at[which, part, i]).wait()

    slot = lax.rem(e, 8)
    spot = pl.ds(pl.multiple_of(slot * CH, CH), CH)
    col_x = lax.rem(q, 4)
    row_y = 2 * h + owner_core

    def device(x, y, core):
        return (2 * z + lax.div(y, 2), 8 * lax.rem(y, 2) + 2 * x + core)

    def wide(x):
        return pl.ds(pl.multiple_of(x * 2 * CH, 2 * CH), 2 * CH)

    def away(t):
        return lax.rem(col_x + t, 4)

    def shard(kind, part, j):
        at = pl.ds(pl.multiple_of(j * CH, CH), CH)
        return wd.at[part, at, :] if kind == 0 else wu.at[part, pl.ds(LOW, RANK - LOW), at]

    def w_remote(kind, t):
        return pltpu.make_async_remote_copy(
            src_ref=(down_in, up_in.at[pl.ds(LOW, RANK - LOW), :])[kind], dst_ref=shard(kind, h, slot),
            send_sem=s_w.at[kind, t], recv_sem=r_w.at[kind, h, c],
            device_id=device(col_x, lax.rem(row_y + t, 4), owner_core), device_id_type=MESH,
        )

    def w_first(kind):
        @pl.when(local)
        def _():
            src = (down_in, up_in.at[pl.ds(LOW, RANK - LOW), :])[kind]
            pltpu.make_async_copy(src, shard(kind, h, slot), r_w.at[kind, h, c]).start()

        @pl.when(jnp.logical_not(local))
        def _():
            w_remote(kind, 0).start()

        for t in (1, 3, 2):
            w_remote(kind, t).start()

    def u_remote(t):
        return pltpu.make_async_remote_copy(
            src_ref=up_in.at[pl.ds(0, LOW), :], dst_ref=wu.at[h, pl.ds(0, LOW), spot],
            send_sem=s_u.at[t], recv_sem=r_u.at[slot],
            device_id=device(away(t), row_y, owner_core), device_id_type=MESH,
        )

    def u_first():
        @pl.when(local)
        def _():
            pltpu.make_async_copy(
                up_in.at[pl.ds(0, LOW), :], wu.at[h, pl.ds(0, LOW), spot], r_u.at[slot]
            ).start()

        @pl.when(jnp.logical_not(local))
        def _():
            u_remote(0).start()

        for t in (1, 3, 2):
            u_remote(t).start()

    def first_start():
        w_first(0)
        u_first()
        w_first(1)

    def first_sent():
        @pl.when(jnp.logical_not(local))
        def _():
            w_remote(0, 0).wait_send()
            w_remote(1, 0).wait_send()
            u_remote(0).wait_send()

        for t in range(1, 4):
            w_remote(0, t).wait_send()
            w_remote(1, t).wait_send()
            u_remote(t).wait_send()

    def w_place(kind, part, x):
        return wd.at[part, wide(x), :] if kind == 0 else wu.at[part, pl.ds(LOW, RANK - LOW), wide(x)]

    def w_block(kind, part, t):
        place = w_place(kind, part, col_x)
        return pltpu.make_async_remote_copy(
            src_ref=place, dst_ref=place, send_sem=s_x.at[kind, part, t], recv_sem=r_x.at[kind, part, col_x],
            device_id=(s, e - 2 * col_x + 2 * away(t)), device_id_type=MESH,
        )

    def w_start(kind, part):
        for j in range(2):
            place = shard(kind, part, 2 * col_x + j)
            pltpu.make_async_copy(place, place, r_w.at[kind, part, j]).wait()
        for t in (1, 3):
            w_block(kind, part, t).start()

    def w_half(kind, part, x, half):
        if kind == 0:
            return wd.at[part, pl.ds(pl.multiple_of((2 * x + half) * CH, CH), CH), :]
        return wu.at[part, pl.ds(LOW + half * ((RANK - LOW) // 2), (RANK - LOW) // 2), wide(x)]

    def w_relay(kind, part, half):
        place = w_half(kind, part, away((3, 1)[half]), half)
        return pltpu.make_async_remote_copy(
            src_ref=place, dst_ref=place, send_sem=s_xr.at[kind, part, half], recv_sem=r_xr.at[kind, part, half],
            device_id=(s, e - 2 * col_x + 2 * away((1, 3)[half])), device_id_type=MESH,
        )

    def w_forward(kind, part):
        for half in range(2):
            x = away((3, 1)[half])
            place = w_place(kind, part, x)
            pltpu.make_async_copy(place, place, r_x.at[kind, part, x]).wait()
            w_relay(kind, part, half).start()

    def u_block(n, t):
        place = wu.at[h, pl.ds(0, LOW), wide(away(n))]
        return pltpu.make_async_remote_copy(
            src_ref=place, dst_ref=place, send_sem=s_v.at[n, t], recv_sem=r_v.at[h, away(n)],
            device_id=device(col_x, lax.rem(row_y + t, 4), c), device_id_type=MESH,
        )

    def u_start(n):
        @pl.when(local)
        def _():
            for j in range(2):
                at = 2 * away(n) + j
                place = wu.at[h, pl.ds(0, LOW), pl.ds(pl.multiple_of(at * CH, CH), CH)]
                pltpu.make_async_copy(place, place, r_u.at[at]).wait()
            for t in (1, 3):
                u_block(n, t).start()

    y_me = 2 * h + lax.div(e, 8)

    def u_half(part, n, half):
        return wu.at[part, pl.ds(pl.multiple_of(half * (LOW // 2), LOW // 2), LOW // 2), wide(away(n))]

    def u_relay(part, n):
        half = jnp.where(lax.rem(y_me - 2 * part - c + 4, 4) == 1, 0, 1)
        place = u_half(part, n, half)
        return pltpu.make_async_remote_copy(
            src_ref=place, dst_ref=place, send_sem=s_vr.at[part, n], recv_sem=r_vr.at[n, half],
            device_id=device(col_x, lax.rem(y_me + 1 + 2 * half, 4), c), device_id_type=MESH,
        )

    def u_forward(n):
        @pl.when(jnp.logical_not(local))
        def _():
            for part in range(2):
                place = wu.at[part, pl.ds(0, LOW), wide(away(n))]
                pltpu.make_async_copy(place, place, r_v.at[part, away(n)]).wait()
                u_relay(part, n).start()

    def weight_wait(kind, part):
        for half in range(2):
            place = w_half(kind, part, away(2), half)
            pltpu.make_async_copy(place, place, r_xr.at[kind, part, half]).wait()
        if kind == 1:
            @pl.when(jnp.logical_and(local, h != part))
            def _():
                for n in range(4):
                    for half in range(2):
                        place = u_half(part, n, half)
                        pltpu.make_async_copy(place, place, r_vr.at[n, half]).wait()

    def weight_sent():
        first_sent()
        for kind in range(2):
            for part in range(2):
                for t in (1, 3):
                    w_block(kind, part, t).wait_send()
                for half in range(2):
                    w_relay(kind, part, half).wait_send()

        @pl.when(local)
        def _():
            for n in range(4):
                for t in (1, 3):
                    u_block(n, t).wait_send()

        @pl.when(jnp.logical_not(local))
        def _():
            for n in range(4):
                for part in range(2):
                    u_relay(part, n).wait_send()

    gain_part = gain_in.at[:, pl.ds(pl.multiple_of(c * HALF, HALF), HALF)]
    gain_near = pltpu.make_async_copy(gain_part, gn.at[h], r_gn.at[h])
    gain_far = pltpu.make_async_remote_copy(
        src_ref=gain_part, dst_ref=gn.at[h], send_sem=s_gn, recv_sem=r_gn.at[h],
        device_id=(s + 1 - 2 * h, e), device_id_type=MESH,
    )

    first_start()
    gain_near.start()
    gain_far.start()
    table_start(0, 0)
    table_start(1, 0)

    @pl.when(z == 0)
    def _():
        end_start(0)

    @pl.when(z == STAGES - 1)
    def _():
        end_start(1)

    w_start(0, h)
    u_start(0)
    w_start(1, h)
    w_start(0, 1 - h)
    w_start(1, 1 - h)
    for n in (1, 3, 2):
        u_start(n)
    w_forward(0, h)
    u_forward(0)
    w_forward(1, h)
    u_forward(1)
    table_start(0, 1)
    table_start(1, 1)
    u_forward(3)
    w_forward(0, 1 - h)
    u_forward(2)
    w_forward(1, 1 - h)
    for part in range(2):
        pltpu.make_async_copy(gn.at[part], gn.at[part], r_gn.at[part]).wait()

    def red_copy(n):
        return pltpu.make_async_remote_copy(
            src_ref=red_tx.at[n], dst_ref=red_rx.at[n], send_sem=s_red.at[n], recv_sem=r_red.at[n],
            device_id=other, device_id_type=MESH,
        )

    def bred_copy(i):
        return pltpu.make_async_remote_copy(
            src_ref=bred_tx.at[i], dst_ref=bred_rx.at[i], send_sem=s_br.at[i], recv_sem=r_br.at[i],
            device_id=other, device_id_type=MESH,
        )

    def one_copy(n):
        src, dst = ((gt_tx, gt_rx), (zed_tx, zed_rx))[n]
        return pltpu.make_async_remote_copy(
            src_ref=src, dst_ref=dst, send_sem=s_one.at[n], recv_sem=r_one.at[n], device_id=other, device_id_type=MESH
        )

    def col(n):
        return slice(n * COLS, (n + 1) * COLS)

    def hop(n, i, ahead):
        rows = pl.ds(pl.multiple_of(i * TOK, TOK), TOK)
        if ahead:
            wide_col = slice(2 * n * COLS, 2 * (n + 1) * COLS)
            src, dst, ss, rs, dev = fout.at[rows, wide_col], xin.at[rows, wide_col], s_hf, r_hf, (s + 2, e)
        else:
            two = pl.ds(2 * n, 2)
            src, dst, ss, rs, dev = bout.at[two, rows, :], uz.at[1, two, rows, pl.ds(0, CH)], s_hb, r_hb, (s - 2, e)
        return pltpu.make_async_remote_copy(
            src_ref=src, dst_ref=dst, send_sem=ss.at[i, n], recv_sem=rs.at[i, n], device_id=dev, device_id_type=MESH
        )

    def rows_copy(kind, b, part, j):
        src = (xz, uz)[kind].at[part, j, pl.ds(pl.multiple_of(b * BATCH, BATCH), BATCH), :]
        return src, landing(kind, b, chip), s_g.at[kind, b, part, j], r_g.at[kind, b, chip], (2 * z + part, 8 * c + j)

    def landing(kind, b, source):
        at = pl.ds(pl.multiple_of((16 * b + source) * BATCH, BATCH), BATCH)
        return (gxz, guz)[kind].at[at, :]

    def rows_each(kind, b, own, far):
        def one(t, carry):
            place = lax.rem(chip + t, 16)
            part, j = lax.div(place, 8), lax.rem(place, 8)
            src, dst, ssem, rsem, dev = rows_copy(kind, b, part, j)
            mine = jnp.logical_and(h == part, 8 * c + j == e)
            if own:
                @pl.when(mine)
                def _():
                    pltpu.make_async_copy(src, dst, rsem).start()

            @pl.when(jnp.logical_not(mine))
            def _():
                far(
                    pltpu.make_async_remote_copy(
                        src_ref=src, dst_ref=dst, send_sem=ssem, recv_sem=rsem, device_id=dev, device_id_type=MESH
                    )
                )

            return carry

        lax.fori_loop(0, 16, one, 0)

    def rows_start(kind, b):
        rows_each(kind, b, True, lambda copy: copy.start())

    def rows_sent(kind, b):
        rows_each(kind, b, False, lambda copy: copy.wait_send())

    def rows_wait(kind, b):
        def one(t, carry):
            place = landing(kind, b, t)
            pltpu.make_async_copy(place, place, r_g.at[kind, b, t]).wait()
            return carry

        lax.fori_loop(0, 16, one, 0)

    def turn():
        for part in range(2):
            def one(j, carry, part=part):
                at = pl.ds(pl.multiple_of(j * CH, CH), CH)
                wdt[part, :, at] = wd[part, at, :].T
                wut[part, at, :] = wu[part, :, at].T
                return carry

            lax.fori_loop(0, HALF // CH, one, 0)

        gt_tx[...] = jnp.zeros_like(gt_tx)

        def product(j, carry):
            at = pl.ds(pl.multiple_of(j * CH, CH), CH)
            gt_tx[...] += nn((wdt[1, :, at].astype(F32) * gn[1, :, at]).astype(BF16), wut[0, at, :])
            return carry

        lax.fori_loop(0, HALF // CH, product, 0)
        one_copy(0).start()
        one_copy(0).wait_recv()
        gt[...] = (gt_tx[...] + gt_rx[...]).astype(BF16)

    late = z >= STAGES // 2

    @pl.when(late)
    def _():
        for kind in range(2):
            for part in range(2):
                weight_wait(kind, part)
        turn()

    def forward(i, carry):
        rows = pl.ds(pl.multiple_of(i * TOK, TOK), TOK)
        fresh = jnp.logical_and(i == 0, jnp.logical_not(late))
        table_wait(0, 0, i)

        @pl.when(i == 0)
        def _():
            table_start(0, 2)
            table_start(1, 2)

        @pl.when(i == 2)
        def _():
            table_start(0, 3)
            table_start(1, 3)


        @pl.when(fresh)
        def _():
            weight_wait(0, 0)

        acc = jnp.zeros((TOK, RANK), F32)
        sq = jnp.zeros((TOK, 128), F32)
        for n in range(NCOL):
            @pl.when(z > 0)
            def _():
                if n % 2 == 0:
                    hop(n // 2, i, True).wait_recv()
                xf[:, col(n)] = rec[0, rows, col(n)].astype(F32) + xin[rows, col(n)].astype(F32)

            @pl.when(z == 0)
            def _():
                xf[:, col(n)] = rec[0, rows, col(n)].astype(F32)

            x = xf[:, col(n)]
            xz[0, n, rows, 0:CH] = x.astype(BF16)
            sq = sq + lanes(x * x)
            acc = acc + nn((x * gn[0, :, col(n)]).astype(BF16), wd[0, col(n), :])

        def finish(part, acc, sq):
            n = 2 * i + part
            red_tx[n, :, 0:RANK] = acc
            red_tx[n, :, RANK:] = sq
            red_copy(n).start()
            red_copy(n).wait_recv()
            total = acc + red_rx[n, :, 0:RANK]
            square = jnp.sum(sq + red_rx[n, :, RANK:], axis=1, keepdims=True)
            scale = lax.rsqrt(square * (1.0 / D) + EPS)
            v = total * scale
            pre[part, rows, :] = v
            scl[part, rows, :] = jnp.broadcast_to(scale, (TOK, 128))
            a = (v * jax.nn.sigmoid(v)).astype(BF16)
            for j in range(8):
                xz[part, j, rows, CH:] = a
            return a

        a = finish(0, acc, sq)

        @pl.when(fresh)
        def _():
            weight_wait(1, 0)
            weight_wait(0, 1)

        table_wait(0, 1, i)
        table_wait(1, 0, i)
        acc = jnp.zeros((TOK, RANK), F32)
        sq = jnp.zeros((TOK, 128), F32)
        for n in range(NCOL):
            x = (
                xf[:, col(n)] + nn(a, wu[0, :, col(n)])
                + (rec[1, rows, col(n)].astype(F32) - sent[0, rows, col(n)].astype(F32))
            )
            xf[:, col(n)] = x
            xz[1, n, rows, 0:CH] = x.astype(BF16)
            sq = sq + lanes(x * x)
            acc = acc + nn((x * gn[1, :, col(n)]).astype(BF16), wd[1, col(n), :])
        a = finish(1, acc, sq)

        @pl.when(fresh)
        def _():
            weight_wait(1, 1)

        table_wait(1, 1, i)

        @pl.when(z < STAGES - 1)
        def _():
            for n in range(NCOL):
                x = xf[:, col(n)] + nn(a, wu[1, :, col(n)]) - sent[1, rows, col(n)].astype(F32)
                fout[rows, col(n)] = x.astype(BF16)
                if n % 2 == 1:
                    hop(n // 2, i, True).start()

        return carry

    lax.fori_loop(0, MB, forward, 0)

    @pl.when(jnp.logical_not(late))
    def _():
        turn()

    zed_tx[...] = jnp.zeros_like(zed_tx)
    for n in range(NCOL):
        zed_tx[...] += nn(xz[1, n, :, 0:CH], wut[0, col(n), :])
    one_copy(1).start()
    one_copy(1).wait_recv()
    zed[...] = zed_tx[...] + zed_rx[...]

    def early():
        def one(b, carry):
            rows_start(0, b)
            return carry

        lax.fori_loop(0, NBATCH, one, 0)

    @pl.when(z < STAGES - 1)
    def _():
        early()

    def backward(i, carry):
        rows = pl.ds(pl.multiple_of(i * TOK, TOK), TOK)

        def slope(part):
            v = pre[part, rows, :]
            gate = jax.nn.sigmoid(v)
            return v, gate * (1.0 + v * (1.0 - gate)), scl[part, rows, 0:1]

        v1, slope1, scale1 = slope(1)
        v0, slope0, scale0 = slope(0)
        acc1 = jnp.zeros((TOK, RANK), F32)
        acc0 = jnp.zeros((TOK, RANK), F32)
        for n in range(NCOL):
            if n % 2 == 0:
                @pl.when(z < STAGES - 1)
                def _():
                    hop(n // 2, i, False).wait_recv()

            @pl.when(z == STAGES - 1)
            def _():
                uz[1, n, rows, 0:CH] = sent[1, rows, col(n)]

            u = uz[1, n, rows, 0:CH]
            acc1 = acc1 + nn(u, wut[1, col(n), :])
            acc0 = acc0 + nn(u, wut[0, col(n), :])
        bred_tx[i, :, 0:RANK] = acc1
        bred_tx[i, :, RANK:] = acc0
        bred_copy(i).start()
        bred_copy(i).wait_recv()

        def finish(d_pre, v, scale):
            mean = jnp.sum(d_pre * v, axis=1, keepdims=True) * (1.0 / D)
            return (d_pre * scale).astype(BF16), mean * scale * scale

        back1, shrink1 = finish((acc1 + bred_rx[i, :, 0:RANK]) * slope1, v1, scale1)
        d_act = acc0 + bred_rx[i, :, RANK:] + nn(back1, gt[...]) - shrink1 * zed[rows, :]
        back0, shrink0 = finish(d_act * slope0, v0, scale0)
        for n in range(NCOL):
            u = (
                uz[1, n, rows, 0:CH].astype(F32) + nn(back1, wdt[1, :, col(n)]) * gn[1, :, col(n)]
                - shrink1 * xz[1, n, rows, 0:CH].astype(F32)
            ).astype(BF16)
            uz[0, n, rows, 0:CH] = u
            uz[1, n, rows, CH:] = back1
            uz[0, n, rows, CH:] = back0
            u = (
                u.astype(F32) + nn(back0, wdt[0, :, col(n)]) * gn[0, :, col(n)]
                - shrink0 * xz[0, n, rows, 0:CH].astype(F32)
            )
            bout[n, rows, :] = u.astype(BF16)
            if n % 2 == 1:
                @pl.when(z > 0)
                def _():
                    hop(n // 2, i, False).start()

        return carry

    def back_batch(b, carry):
        lax.fori_loop(b * (BATCH // TOK), (b + 1) * (BATCH // TOK), backward, 0)
        rows_start(1, b)
        return carry

    lax.fori_loop(0, NBATCH, back_batch, 0)

    @pl.when(z == STAGES - 1)
    def _():
        early()

    gd_out[...] = jnp.zeros_like(gd_out)
    gu_out[...] = jnp.zeros_like(gu_out)

    def total(b, carry):
        rows_wait(0, b)
        rows_wait(1, b)
        at = pl.ds(pl.multiple_of(16 * BATCH * b, 16 * BATCH), 16 * BATCH)
        gd_out[...] += tn(gxz[at, 0:CH], guz[at, CH:])
        gu_out[...] += tn(gxz[at, CH:], guz[at, 0:CH])
        return carry

    lax.fori_loop(0, NBATCH, total, 0)

    def all_rows_sent(b, carry):
        rows_sent(0, b)
        rows_sent(1, b)
        return carry

    lax.fori_loop(0, NBATCH, all_rows_sent, 0)
    weight_sent()
    gain_far.wait_send()

    @pl.when(z == 0)
    def _():
        end_sent(0)

    @pl.when(z == STAGES - 1)
    def _():
        end_sent(1)

    for k in range(4):
        table_sent(0, k)
        table_sent(1, k)

    def rest(i, carry):
        for n in range(NCOL // 2):
            @pl.when(z < STAGES - 1)
            def _():
                hop(n, i, True).wait_send()

            @pl.when(z > 0)
            def _():
                hop(n, i, False).wait_send()

        for k in range(2):
            red_copy(2 * i + k).wait_send()
        bred_copy(i).wait_send()
        return carry

    lax.fori_loop(0, MB, rest, 0)
    one_copy(0).wait_send()
    one_copy(1).wait_send()


def shards(tokens, cotangent, sample_ids, sent_before, received_before, norm_gain, down_proj, up_proj):
    e = lax.axis_index("dp")
    gain = lax.dynamic_slice(norm_gain[0], (e * CH,), (CH,))[:, None]
    any_ = pl.BlockSpec(memory_space=pl.ANY)
    vmem = pl.BlockSpec(memory_space=pltpu.VMEM)
    dma = pltpu.SemaphoreType.DMA
    rows = MB * TOK
    grad_down, grad_up = pl.pallas_call(
        kernel,
        out_shape=(jax.ShapeDtypeStruct((CH, RANK), F32), jax.ShapeDtypeStruct((RANK, CH), F32)),
        in_specs=[pl.BlockSpec(memory_space=pltpu.SMEM)] + [any_] * 7,
        out_specs=(vmem, vmem),
        scratch_shapes=[
            pltpu.VMEM((MB, TOK, D), BF16),
            pltpu.VMEM((4, TOK, D), BF16),
            pltpu.VMEM((2, 1, HALF), F32),
            pltpu.VMEM((2, rows, HALF), BF16),
            pltpu.VMEM((2, rows, HALF), BF16),
            pltpu.VMEM((2, HALF, RANK), BF16),
            pltpu.VMEM((2, RANK, HALF), BF16),
            pltpu.VMEM((2, RANK, HALF), BF16),
            pltpu.VMEM((2, HALF, RANK), BF16),
            pltpu.VMEM((rows, HALF), BF16),
            pltpu.VMEM((2, 8, rows, PACK), BF16),
            pltpu.VMEM((2, 8, rows, PACK), BF16),
            pltpu.VMEM((TOK, HALF), F32),
            pltpu.VMEM((rows, HALF), BF16),
            pltpu.VMEM((8, rows, CH), BF16),
            pltpu.VMEM((2 * MB, TOK, RANK + 128), F32),
            pltpu.VMEM((2 * MB, TOK, RANK + 128), F32),
            pltpu.VMEM((MB, TOK, 2 * RANK), F32),
            pltpu.VMEM((MB, TOK, 2 * RANK), F32),
            pltpu.VMEM((RANK, RANK), F32),
            pltpu.VMEM((RANK, RANK), F32),
            pltpu.VMEM((rows, RANK), F32),
            pltpu.VMEM((rows, RANK), F32),
            pltpu.VMEM((RANK, RANK), BF16),
            pltpu.VMEM((rows, RANK), F32),
            pltpu.VMEM((2, rows, RANK), F32),
            pltpu.VMEM((2, rows, 128), F32),
            pltpu.VMEM((16 * rows, PACK), BF16),
            pltpu.VMEM((16 * rows, PACK), BF16),
            dma, dma((4,)),
            dma, dma((2,)),
            dma((2, 4, 4)), dma((2, 2, MB)),
            dma((2, 4)), dma((2, 2, 2)), dma((2, 2, 4)), dma((2, 2, 4)), dma((2, 2, 2)), dma((2, 2, 2)),
            dma((4,)), dma((8,)), dma((4, 4)), dma((2, 4)), dma((2, 4)), dma((4, 2)),
            dma((MB, NCOL // 2)), dma((MB, NCOL // 2)),
            dma((MB, NCOL // 2)), dma((MB, NCOL // 2)),
            dma((2 * MB,)), dma((2 * MB,)), dma((MB,)), dma((MB,)), dma((2,)), dma((2,)),
            dma((2, NBATCH, 2, 8)), dma((2, NBATCH, 16)),
        ],
        compiler_params=pltpu.CompilerParams(
            collective_id=0, has_side_effects=True, vmem_limit_bytes=56 * 1024 * 1024
        ),
    )(sample_ids, received_before[0], sent_before[0], tokens, cotangent, norm_gain, down_proj[0], up_proj[0])
    return ((grad_down * gain)[None], grad_up[None])


def solution(mesh):
    placed = (
        P(None, "dp", None),
        P(None, "dp", None),
        P("dp", None),
        P("section", "dp", None, None),
        P("section", "dp", None, None),
        P("section", None),
        P("section", "dp", None),
        P("section", None, "dp"),
    )
    return jax.shard_map(
        shards,
        mesh=mesh,
        in_specs=placed,
        out_specs=(P("section", "dp", None), P("section", None, "dp")),
        check_vma=False,
    )
```

```python
import functools

import jax
import jax.numpy as jnp
from jax import lax
from jax.experimental import pallas as pl
from jax.experimental.pallas import tpu as pltpu
from jax.sharding import PartitionSpec as P

MESH = pl.DeviceIdType.MESH
F32, BF16 = jnp.float32, jnp.bfloat16
EPS = 1e-05
D = 8192
HALF = 4096
RANK = 256
TOK = 16
MB = 8
CH = 512
COLS = 512
NCOL = HALF // COLS
STAGES = 8
BATCH = 2 * TOK
NBATCH = MB * TOK // BATCH
PACK = CH + RANK
LOW = 128


def tn(a, b):
    return lax.dot_general(a, b, (((0,), (0,)), ((), ())), preferred_element_type=F32)


def nn(a, b):
    return jnp.dot(a, b, preferred_element_type=F32)


def lanes(v):
    total = v[:, 0:128]
    for k in range(128, v.shape[1], 128):
        total = total + v[:, k : k + 128]
    return total


def kernel(
    ids, rec_in, sent_in, tok_in, cot_in, gain_in, down_in, up_in, gd_out, gu_out,
    raw, perm, gn, rec, sent, wd, wu, wdt, wut, xin, xz, uz, xf, fout, bout, red_tx, red_rx,
    bred_tx, bred_rx, gt_tx, gt_rx, zed_tx, zed_rx, gt, zed, pre, scl, gxz, guz,
    c_raw, s_tok, s_gn, r_gn, s_tab, r_tab, s_w, r_w, s_x, r_x, s_xr, r_xr,
    s_u, r_u, s_v, r_v, s_vr, r_vr,
    s_hf, r_hf, s_hb, r_hb, s_red, r_red, s_br, r_br, s_one, r_one, s_g, r_g,
):
    s = lax.axis_index("section")
    e = lax.axis_index("dp")
    h, z = lax.rem(s, 2), lax.div(s, 2)
    c, q = lax.rem(e, 2), lax.div(e, 2)
    chip = h * 8 + q
    owner_core = lax.div(e, 8)
    local = c == owner_core
    other = (s, e + 1 - 2 * c)

    raw_tok = pltpu.make_async_copy(tok_in, raw, c_raw)
    raw_cot = pltpu.make_async_copy(cot_in, raw, c_raw)

    @pl.when(z == 0)
    def _():
        raw_tok.start()

    @pl.when(z == STAGES - 1)
    def _():
        raw_cot.start()

    barrier = pltpu.get_barrier_semaphore()

    def greet(t, carry):
        place = lax.rem(h * 16 + e + t, 32)
        pl.semaphore_signal(
            barrier, inc=1, device_id=(2 * z + lax.div(place, 16), lax.rem(place, 16)), device_id_type=MESH
        )
        return carry

    lax.fori_loop(1, 32, greet, 0)

    @pl.when(z > 0)
    def _():
        pl.semaphore_signal(barrier, inc=1, device_id=(s - 2, e), device_id_type=MESH)

    @pl.when(z < STAGES - 1)
    def _():
        pl.semaphore_signal(barrier, inc=1, device_id=(s + 2, e), device_id_type=MESH)

    neighbours = jnp.where(z > 0, 1, 0) + jnp.where(z < STAGES - 1, 1, 0)
    pl.semaphore_wait(barrier, 31 + neighbours)

    def table_copy(which, k, t):
        src = (rec_in, sent_in)[which]
        dst = (rec, sent)[which]
        h2, c2 = lax.rem(h + t // 2, 2), lax.rem(c + t, 2)
        row = pl.multiple_of((2 * k + c) * TOK, TOK)
        return dict(
            src_ref=src.at[4 * h2 + k, :, pl.ds(pl.multiple_of(c2 * HALF, HALF), HALF)],
            dst_ref=dst.at[h, pl.ds(row, TOK), :],
        ), s_tab.at[which, k, t], r_tab.at[which, h, 2 * k + c], (2 * z + h2, 2 * q + c2)

    def table_used(which):
        return s != (0, 2 * STAGES - 1)[which]

    def table_start(which, k):
        @pl.when(table_used(which))
        def _():
            for t in range(4):
                refs, ssem, rsem, dev = table_copy(which, k, t)
                if t == 0:
                    pltpu.make_async_copy(refs["src_ref"], refs["dst_ref"], rsem).start()
                else:
                    pltpu.make_async_remote_copy(
                        **refs, send_sem=ssem, recv_sem=rsem, device_id=dev, device_id_type=MESH
                    ).start()

    def table_sent(which, k):
        @pl.when(table_used(which))
        def _():
            for t in range(1, 4):
                refs, ssem, rsem, dev = table_copy(which, k, t)
                pltpu.make_async_remote_copy(
                    **refs, send_sem=ssem, recv_sem=rsem, device_id=dev, device_id_type=MESH
                ).wait_send()

    def end_copies(which, k):
        dst, part = ((rec, 0), (sent, 1))[which]
        place = dst.at[part, pl.ds(pl.multiple_of((2 * k + c) * TOK, TOK), TOK), :]
        rsem = r_tab.at[which, part, 2 * k + c]
        mine = perm.at[k, :, pl.ds(pl.multiple_of(c * HALF, HALF), HALF)]
        return mine, place, rsem

    def end_far(which, k):
        theirs = perm.at[k, :, pl.ds(pl.multiple_of((1 - c) * HALF, HALF), HALF)]
        place, rsem = end_copies(which, k)[1:]
        return pltpu.make_async_remote_copy(
            src_ref=theirs, dst_ref=place, send_sem=s_tok.at[k], recv_sem=rsem, device_id=other, device_id_type=MESH
        )

    def end_start(which):
        (raw_tok, raw_cot)[which].wait()
        for k in range(4):
            at = jnp.int32(0)
            for m in range(1, MB):
                at = jnp.where(ids[0, m] == 4 * h + k, m, at)
            at = jnp.clip(at, 0, MB - 1)

            def move(n, carry, at=at, k=k):
                cols = pl.ds(pl.multiple_of(n * 1024, 1024), 1024)
                perm[k, :, cols] = raw[at, :, cols]
                return carry

            lax.fori_loop(0, D // 1024, move, 0)
            end_far(which, k).start()
            pltpu.make_async_copy(*end_copies(which, k)).start()

    def end_sent(which):
        for k in range(4):
            end_far(which, k).wait_send()

    def table_wait(which, part, i):
        place = (rec, sent)[which].at[part, pl.ds(pl.multiple_of(i * TOK, TOK), TOK), :]
        pltpu.make_async_copy(place, place, r_tab.at[which, part, i]).wait()

    slot = lax.rem(e, 8)
    spot = pl.ds(pl.multiple_of(slot * CH, CH), CH)
    col_x = lax.rem(q, 4)
    row_y = 2 * h + owner_core

    def device(x, y, core):
        return (2 * z + lax.div(y, 2), 8 * lax.rem(y, 2) + 2 * x + core)

    def wide(x):
        return pl.ds(pl.multiple_of(x * 2 * CH, 2 * CH), 2 * CH)

    def away(t):
        return lax.rem(col_x + t, 4)

    def shard(kind, part, j):
        at = pl.ds(pl.multiple_of(j * CH, CH), CH)
        return wd.at[part, at, :] if kind == 0 else wu.at[part, pl.ds(LOW, RANK - LOW), at]

    def w_remote(kind, t):
        return pltpu.make_async_remote_copy(
            src_ref=(down_in, up_in.at[pl.ds(LOW, RANK - LOW), :])[kind], dst_ref=shard(kind, h, slot),
            send_sem=s_w.at[kind, t], recv_sem=r_w.at[kind, h, c],
            device_id=device(col_x, lax.rem(row_y + t, 4), owner_core), device_id_type=MESH,
        )

    def w_first(kind):
        @pl.when(local)
        def _():
            src = (down_in, up_in.at[pl.ds(LOW, RANK - LOW), :])[kind]
            pltpu.make_async_copy(src, shard(kind, h, slot), r_w.at[kind, h, c]).start()

        @pl.when(jnp.logical_not(local))
        def _():
            w_remote(kind, 0).start()

        for t in (1, 3, 2):
            w_remote(kind, t).start()

    def u_remote(t):
        return pltpu.make_async_remote_copy(
            src_ref=up_in.at[pl.ds(0, LOW), :], dst_ref=wu.at[h, pl.ds(0, LOW), spot],
            send_sem=s_u.at[t], recv_sem=r_u.at[slot],
            device_id=device(away(t), row_y, owner_core), device_id_type=MESH,
        )

    def u_first():
        @pl.when(local)
        def _():
            pltpu.make_async_copy(
                up_in.at[pl.ds(0, LOW), :], wu.at[h, pl.ds(0, LOW), spot], r_u.at[slot]
            ).start()

        @pl.when(jnp.logical_not(local))
        def _():
            u_remote(0).start()

        for t in (1, 3, 2):
            u_remote(t).start()

    def first_start():
        w_first(0)
        u_first()
        w_first(1)

    def first_sent():
        @pl.when(jnp.logical_not(local))
        def _():
            w_remote(0, 0).wait_send()
            w_remote(1, 0).wait_send()
            u_remote(0).wait_send()

        for t in range(1, 4):
            w_remote(0, t).wait_send()
            w_remote(1, t).wait_send()
            u_remote(t).wait_send()

    def w_place(kind, part, x):
        return wd.at[part, wide(x), :] if kind == 0 else wu.at[part, pl.ds(LOW, RANK - LOW), wide(x)]

    def w_block(kind, part, t):
        place = w_place(kind, part, col_x)
        return pltpu.make_async_remote_copy(
            src_ref=place, dst_ref=place, send_sem=s_x.at[kind, part, t], recv_sem=r_x.at[kind, part, col_x],
            device_id=(s, e - 2 * col_x + 2 * away(t)), device_id_type=MESH,
        )

    def w_start(kind, part):
        for j in range(2):
            place = shard(kind, part, 2 * col_x + j)
            pltpu.make_async_copy(place, place, r_w.at[kind, part, j]).wait()
        for t in (1, 3):
            w_block(kind, part, t).start()

    def w_half(kind, part, x, half):
        if kind == 0:
            return wd.at[part, pl.ds(pl.multiple_of((2 * x + half) * CH, CH), CH), :]
        return wu.at[part, pl.ds(LOW + half * ((RANK - LOW) // 2), (RANK - LOW) // 2), wide(x)]

    def w_relay(kind, part, half):
        place = w_half(kind, part, away((3, 1)[half]), half)
        return pltpu.make_async_remote_copy(
            src_ref=place, dst_ref=place, send_sem=s_xr.at[kind, part, half], recv_sem=r_xr.at[kind, part, half],
            device_id=(s, e - 2 * col_x + 2 * away((1, 3)[half])), device_id_type=MESH,
        )

    def w_forward(kind, part):
        for half in range(2):
            x = away((3, 1)[half])
            place = w_place(kind, part, x)
            pltpu.make_async_copy(place, place, r_x.at[kind, part, x]).wait()
            w_relay(kind, part, half).start()

    def u_block(n, t):
        place = wu.at[h, pl.ds(0, LOW), wide(away(n))]
        return pltpu.make_async_remote_copy(
            src_ref=place, dst_ref=place, send_sem=s_v.at[n, t], recv_sem=r_v.at[h, away(n)],
            device_id=device(col_x, lax.rem(row_y + t, 4), c), device_id_type=MESH,
        )

    def u_start(n):
        @pl.when(local)
        def _():
            for j in range(2):
                at = 2 * away(n) + j
                place = wu.at[h, pl.ds(0, LOW), pl.ds(pl.multiple_of(at * CH, CH), CH)]
                pltpu.make_async_copy(place, place, r_u.at[at]).wait()
            for t in (1, 3):
                u_block(n, t).start()

    y_me = 2 * h + lax.div(e, 8)

    def u_half(part, n, half):
        return wu.at[part, pl.ds(pl.multiple_of(half * (LOW // 2), LOW // 2), LOW // 2), wide(away(n))]

    def u_relay(part, n):
        half = jnp.where(lax.rem(y_me - 2 * part - c + 4, 4) == 1, 0, 1)
        place = u_half(part, n, half)
        return pltpu.make_async_remote_copy(
            src_ref=place, dst_ref=place, send_sem=s_vr.at[part, n], recv_sem=r_vr.at[n, half],
            device_id=device(col_x, lax.rem(y_me + 1 + 2 * half, 4), c), device_id_type=MESH,
        )

    def u_forward(n):
        @pl.when(jnp.logical_not(local))
        def _():
            for part in range(2):
                place = wu.at[part, pl.ds(0, LOW), wide(away(n))]
                pltpu.make_async_copy(place, place, r_v.at[part, away(n)]).wait()
                u_relay(part, n).start()

    def weight_wait(kind, part):
        for half in range(2):
            place = w_half(kind, part, away(2), half)
            pltpu.make_async_copy(place, place, r_xr.at[kind, part, half]).wait()
        if kind == 1:
            @pl.when(jnp.logical_and(local, h != part))
            def _():
                for n in range(4):
                    for half in range(2):
                        place = u_half(part, n, half)
                        pltpu.make_async_copy(place, place, r_vr.at[n, half]).wait()

    def weight_sent():
        first_sent()
        for kind in range(2):
            for part in range(2):
                for t in (1, 3):
                    w_block(kind, part, t).wait_send()
                for half in range(2):
                    w_relay(kind, part, half).wait_send()

        @pl.when(local)
        def _():
            for n in range(4):
                for t in (1, 3):
                    u_block(n, t).wait_send()

        @pl.when(jnp.logical_not(local))
        def _():
            for n in range(4):
                for part in range(2):
                    u_relay(part, n).wait_send()

    gain_part = gain_in.at[:, pl.ds(pl.multiple_of(c * HALF, HALF), HALF)]
    gain_near = pltpu.make_async_copy(gain_part, gn.at[h], r_gn.at[h])
    gain_far = pltpu.make_async_remote_copy(
        src_ref=gain_part, dst_ref=gn.at[h], send_sem=s_gn, recv_sem=r_gn.at[h],
        device_id=(s + 1 - 2 * h, e), device_id_type=MESH,
    )

    first_start()
    gain_near.start()
    gain_far.start()
    table_start(0, 0)
    table_start(1, 0)

    @pl.when(z == 0)
    def _():
        end_start(0)

    @pl.when(z == STAGES - 1)
    def _():
        end_start(1)

    w_start(0, h)
    u_start(0)
    w_start(1, h)
    w_start(0, 1 - h)
    w_start(1, 1 - h)
    for n in (1, 3, 2):
        u_start(n)
    w_forward(0, h)
    u_forward(0)
    w_forward(1, h)
    u_forward(1)
    table_start(0, 1)
    table_start(1, 1)
    u_forward(3)
    w_forward(0, 1 - h)
    u_forward(2)
    w_forward(1, 1 - h)
    for part in range(2):
        pltpu.make_async_copy(gn.at[part], gn.at[part], r_gn.at[part]).wait()

    def red_copy(n):
        return pltpu.make_async_remote_copy(
            src_ref=red_tx.at[n], dst_ref=red_rx.at[n], send_sem=s_red.at[n], recv_sem=r_red.at[n],
            device_id=other, device_id_type=MESH,
        )

    def bred_copy(i):
        return pltpu.make_async_remote_copy(
            src_ref=bred_tx.at[i], dst_ref=bred_rx.at[i], send_sem=s_br.at[i], recv_sem=r_br.at[i],
            device_id=other, device_id_type=MESH,
        )

    def one_copy(n):
        src, dst = ((gt_tx, gt_rx), (zed_tx, zed_rx))[n]
        return pltpu.make_async_remote_copy(
            src_ref=src, dst_ref=dst, send_sem=s_one.at[n], recv_sem=r_one.at[n], device_id=other, device_id_type=MESH
        )

    def col(n):
        return slice(n * COLS, (n + 1) * COLS)

    def hop(n, i, ahead):
        rows = pl.ds(pl.multiple_of(i * TOK, TOK), TOK)
        if ahead:
            wide_col = slice(2 * n * COLS, 2 * (n + 1) * COLS)
            src, dst, ss, rs, dev = fout.at[rows, wide_col], xin.at[rows, wide_col], s_hf, r_hf, (s + 2, e)
        else:
            two = pl.ds(2 * n, 2)
            src, dst, ss, rs, dev = bout.at[two, rows, :], uz.at[1, two, rows, pl.ds(0, CH)], s_hb, r_hb, (s - 2, e)
        return pltpu.make_async_remote_copy(
            src_ref=src, dst_ref=dst, send_sem=ss.at[i, n], recv_sem=rs.at[i, n], device_id=dev, device_id_type=MESH
        )

    def rows_copy(kind, b, part, j):
        src = (xz, uz)[kind].at[part, j, pl.ds(pl.multiple_of(b * BATCH, BATCH), BATCH), :]
        return src, landing(kind, b, chip), s_g.at[kind, b, part, j], r_g.at[kind, b, chip], (2 * z + part, 8 * c + j)

    def landing(kind, b, source):
        at = pl.ds(pl.multiple_of((16 * b + source) * BATCH, BATCH), BATCH)
        return (gxz, guz)[kind].at[at, :]

    def rows_each(kind, b, own, far):
        def one(t, carry):
            place = lax.rem(chip + t, 16)
            part, j = lax.div(place, 8), lax.rem(place, 8)
            src, dst, ssem, rsem, dev = rows_copy(kind, b, part, j)
            mine = jnp.logical_and(h == part, 8 * c + j == e)
            if own:
                @pl.when(mine)
                def _():
                    pltpu.make_async_copy(src, dst, rsem).start()

            @pl.when(jnp.logical_not(mine))
            def _():
                far(
                    pltpu.make_async_remote_copy(
                        src_ref=src, dst_ref=dst, send_sem=ssem, recv_sem=rsem, device_id=dev, device_id_type=MESH
                    )
                )

            return carry

        lax.fori_loop(0, 16, one, 0, unroll=4)

    def rows_start(kind, b):
        rows_each(kind, b, True, lambda copy: copy.start())

    def rows_sent(kind, b):
        rows_each(kind, b, False, lambda copy: copy.wait_send())

    def rows_wait(kind, b):
        def one(t, carry):
            place = landing(kind, b, t)
            pltpu.make_async_copy(place, place, r_g.at[kind, b, t]).wait()
            return carry

        lax.fori_loop(0, 16, one, 0)

    def turn():
        for part in range(2):
            def one(j, carry, part=part):
                at = pl.ds(pl.multiple_of(j * CH, CH), CH)
                wdt[part, :, at] = wd[part, at, :].T
                wut[part, at, :] = wu[part, :, at].T
                return carry

            lax.fori_loop(0, HALF // CH, one, 0)

        gt_tx[...] = jnp.zeros_like(gt_tx)

        def product(j, carry):
            at = pl.ds(pl.multiple_of(j * CH, CH), CH)
            gt_tx[...] += nn((wdt[1, :, at].astype(F32) * gn[1, :, at]).astype(BF16), wut[0, at, :])
            return carry

        lax.fori_loop(0, HALF // CH, product, 0)
        one_copy(0).start()
        one_copy(0).wait_recv()
        gt[...] = (gt_tx[...] + gt_rx[...]).astype(BF16)

    late = z >= STAGES // 2

    @pl.when(late)
    def _():
        for kind in range(2):
            for part in range(2):
                weight_wait(kind, part)
        turn()

    def forward(i, carry):
        rows = pl.ds(pl.multiple_of(i * TOK, TOK), TOK)
        fresh = jnp.logical_and(i == 0, jnp.logical_not(late))
        table_wait(0, 0, i)

        @pl.when(i == 0)
        def _():
            table_start(0, 2)
            table_start(1, 2)

        @pl.when(i == 2)
        def _():
            table_start(0, 3)
            table_start(1, 3)


        @pl.when(fresh)
        def _():
            weight_wait(0, 0)

        acc = jnp.zeros((TOK, RANK), F32)
        sq = jnp.zeros((TOK, 128), F32)
        for n in range(NCOL):
            @pl.when(z > 0)
            def _():
                if n % 2 == 0:
                    hop(n // 2, i, True).wait_recv()
                xf[:, col(n)] = rec[0, rows, col(n)].astype(F32) + xin[rows, col(n)].astype(F32)

            @pl.when(z == 0)
            def _():
                xf[:, col(n)] = rec[0, rows, col(n)].astype(F32)

            x = xf[:, col(n)]
            xz[0, n, rows, 0:CH] = x.astype(BF16)
            sq = sq + lanes(x * x)
            acc = acc + nn((x * gn[0, :, col(n)]).astype(BF16), wd[0, col(n), :])

        def finish(part, acc, sq):
            n = 2 * i + part
            red_tx[n, :, 0:RANK] = acc
            red_tx[n, :, RANK:] = sq
            red_copy(n).start()
            red_copy(n).wait_recv()
            total = acc + red_rx[n, :, 0:RANK]
            square = jnp.sum(sq + red_rx[n, :, RANK:], axis=1, keepdims=True)
            scale = lax.rsqrt(square * (1.0 / D) + EPS)
            v = total * scale
            pre[part, rows, :] = v
            scl[part, rows, :] = jnp.broadcast_to(scale, (TOK, 128))
            a = (v * jax.nn.sigmoid(v)).astype(BF16)
            for j in range(8):
                xz[part, j, rows, CH:] = a
            return a

        a = finish(0, acc, sq)

        @pl.when(fresh)
        def _():
            weight_wait(1, 0)
            weight_wait(0, 1)

        table_wait(0, 1, i)
        table_wait(1, 0, i)
        acc = jnp.zeros((TOK, RANK), F32)
        sq = jnp.zeros((TOK, 128), F32)
        for n in range(NCOL):
            x = (
                xf[:, col(n)] + nn(a, wu[0, :, col(n)])
                + (rec[1, rows, col(n)].astype(F32) - sent[0, rows, col(n)].astype(F32))
            )
            xf[:, col(n)] = x
            xz[1, n, rows, 0:CH] = x.astype(BF16)
            sq = sq + lanes(x * x)
            acc = acc + nn((x * gn[1, :, col(n)]).astype(BF16), wd[1, col(n), :])
        a = finish(1, acc, sq)

        @pl.when(fresh)
        def _():
            weight_wait(1, 1)

        table_wait(1, 1, i)

        @pl.when(z < STAGES - 1)
        def _():
            for n in range(NCOL):
                x = xf[:, col(n)] + nn(a, wu[1, :, col(n)]) - sent[1, rows, col(n)].astype(F32)
                fout[rows, col(n)] = x.astype(BF16)
                if n % 2 == 1:
                    hop(n // 2, i, True).start()

        return carry

    lax.fori_loop(0, MB, forward, 0)

    @pl.when(jnp.logical_not(late))
    def _():
        turn()

    zed_tx[...] = jnp.zeros_like(zed_tx)
    for n in range(NCOL):
        zed_tx[...] += nn(xz[1, n, :, 0:CH], wut[0, col(n), :])
    one_copy(1).start()

    def early():
        def one(b, carry):
            rows_start(0, b)
            return carry

        lax.fori_loop(0, NBATCH, one, 0)

    @pl.when(z < STAGES - 1)
    def _():
        early()

    def backward(i, carry):
        rows = pl.ds(pl.multiple_of(i * TOK, TOK), TOK)

        def slope(part):
            v = pre[part, rows, :]
            gate = jax.nn.sigmoid(v)
            return v, gate * (1.0 + v * (1.0 - gate)), scl[part, rows, 0:1]

        v1, slope1, scale1 = slope(1)
        v0, slope0, scale0 = slope(0)
        acc1 = jnp.zeros((TOK, RANK), F32)
        acc0 = jnp.zeros((TOK, RANK), F32)
        for n in range(NCOL):
            if n % 2 == 0:
                @pl.when(z < STAGES - 1)
                def _():
                    hop(n // 2, i, False).wait_recv()

            @pl.when(z == STAGES - 1)
            def _():
                uz[1, n, rows, 0:CH] = sent[1, rows, col(n)]

            u = uz[1, n, rows, 0:CH]
            acc1 = acc1 + nn(u, wut[1, col(n), :])
            acc0 = acc0 + nn(u, wut[0, col(n), :])
        bred_tx[i, :, 0:RANK] = acc1
        bred_tx[i, :, RANK:] = acc0
        bred_copy(i).start()

        @pl.when(i == 0)
        def _():
            one_copy(1).wait_recv()
            zed[...] = zed_tx[...] + zed_rx[...]

        bred_copy(i).wait_recv()

        def finish(d_pre, v, scale):
            mean = jnp.sum(d_pre * v, axis=1, keepdims=True) * (1.0 / D)
            return (d_pre * scale).astype(BF16), mean * scale * scale

        back1, shrink1 = finish((acc1 + bred_rx[i, :, 0:RANK]) * slope1, v1, scale1)
        d_act = acc0 + bred_rx[i, :, RANK:] + nn(back1, gt[...]) - shrink1 * zed[rows, :]
        back0, shrink0 = finish(d_act * slope0, v0, scale0)
        for n in range(NCOL):
            u = (
                uz[1, n, rows, 0:CH].astype(F32) + nn(back1, wdt[1, :, col(n)]) * gn[1, :, col(n)]
                - shrink1 * xz[1, n, rows, 0:CH].astype(F32)
            ).astype(BF16)
            uz[0, n, rows, 0:CH] = u
            uz[1, n, rows, CH:] = back1
            uz[0, n, rows, CH:] = back0
            u = (
                u.astype(F32) + nn(back0, wdt[0, :, col(n)]) * gn[0, :, col(n)]
                - shrink0 * xz[0, n, rows, 0:CH].astype(F32)
            )
            bout[n, rows, :] = u.astype(BF16)
            if n % 2 == 1:
                @pl.when(z > 0)
                def _():
                    hop(n // 2, i, False).start()

        return carry

    def back_batch(b, carry):
        lax.fori_loop(b * (BATCH // TOK), (b + 1) * (BATCH // TOK), backward, 0)
        rows_start(1, b)
        return carry

    lax.fori_loop(0, NBATCH, back_batch, 0)

    @pl.when(z == STAGES - 1)
    def _():
        early()

    weight_sent()
    gain_far.wait_send()

    @pl.when(z == 0)
    def _():
        end_sent(0)

    @pl.when(z == STAGES - 1)
    def _():
        end_sent(1)

    for k in range(4):
        table_sent(0, k)
        table_sent(1, k)

    def rest(i, carry):
        for n in range(NCOL // 2):
            @pl.when(z < STAGES - 1)
            def _():
                hop(n, i, True).wait_send()

            @pl.when(z > 0)
            def _():
                hop(n, i, False).wait_send()

        for k in range(2):
            red_copy(2 * i + k).wait_send()
        bred_copy(i).wait_send()
        return carry

    lax.fori_loop(0, MB, rest, 0)
    one_copy(0).wait_send()
    one_copy(1).wait_send()

    def rows_gone(b, carry):
        rows_sent(0, b)

        @pl.when(b < NBATCH - 1)
        def _():
            rows_sent(1, b)

        return carry

    lax.fori_loop(0, NBATCH, rows_gone, 0)

    gd_out[...] = jnp.zeros_like(gd_out)
    gu_out[...] = jnp.zeros_like(gu_out)

    def total(b, carry):
        rows_wait(0, b)
        rows_wait(1, b)
        at = pl.ds(pl.multiple_of(16 * BATCH * b, 16 * BATCH), 16 * BATCH)
        gd_out[...] += tn(gxz[at, 0:CH], guz[at, CH:])
        gu_out[...] += tn(gxz[at, CH:], guz[at, 0:CH])
        return carry

    lax.fori_loop(0, NBATCH, total, 0)
    rows_sent(1, NBATCH - 1)


def shards(tokens, cotangent, sample_ids, sent_before, received_before, norm_gain, down_proj, up_proj):
    e = lax.axis_index("dp")
    gain = lax.dynamic_slice(norm_gain[0], (e * CH,), (CH,))[:, None]
    any_ = pl.BlockSpec(memory_space=pl.ANY)
    vmem = pl.BlockSpec(memory_space=pltpu.VMEM)
    dma = pltpu.SemaphoreType.DMA
    rows = MB * TOK
    grad_down, grad_up = pl.pallas_call(
        kernel,
        out_shape=(jax.ShapeDtypeStruct((CH, RANK), F32), jax.ShapeDtypeStruct((RANK, CH), F32)),
        in_specs=[pl.BlockSpec(memory_space=pltpu.SMEM)] + [any_] * 7,
        out_specs=(vmem, vmem),
        scratch_shapes=[
            pltpu.VMEM((MB, TOK, D), BF16),
            pltpu.VMEM((4, TOK, D), BF16),
            pltpu.VMEM((2, 1, HALF), F32),
            pltpu.VMEM((2, rows, HALF), BF16),
            pltpu.VMEM((2, rows, HALF), BF16),
            pltpu.VMEM((2, HALF, RANK), BF16),
            pltpu.VMEM((2, RANK, HALF), BF16),
            pltpu.VMEM((2, RANK, HALF), BF16),
            pltpu.VMEM((2, HALF, RANK), BF16),
            pltpu.VMEM((rows, HALF), BF16),
            pltpu.VMEM((2, 8, rows, PACK), BF16),
            pltpu.VMEM((2, 8, rows, PACK), BF16),
            pltpu.VMEM((TOK, HALF), F32),
            pltpu.VMEM((rows, HALF), BF16),
            pltpu.VMEM((8, rows, CH), BF16),
            pltpu.VMEM((2 * MB, TOK, RANK + 128), F32),
            pltpu.VMEM((2 * MB, TOK, RANK + 128), F32),
            pltpu.VMEM((MB, TOK, 2 * RANK), F32),
            pltpu.VMEM((MB, TOK, 2 * RANK), F32),
            pltpu.VMEM((RANK, RANK), F32),
            pltpu.VMEM((RANK, RANK), F32),
            pltpu.VMEM((rows, RANK), F32),
            pltpu.VMEM((rows, RANK), F32),
            pltpu.VMEM((RANK, RANK), BF16),
            pltpu.VMEM((rows, RANK), F32),
            pltpu.VMEM((2, rows, RANK), F32),
            pltpu.VMEM((2, rows, 128), F32),
            pltpu.VMEM((16 * rows, PACK), BF16),
            pltpu.VMEM((16 * rows, PACK), BF16),
            dma, dma((4,)),
            dma, dma((2,)),
            dma((2, 4, 4)), dma((2, 2, MB)),
            dma((2, 4)), dma((2, 2, 2)), dma((2, 2, 4)), dma((2, 2, 4)), dma((2, 2, 2)), dma((2, 2, 2)),
            dma((4,)), dma((8,)), dma((4, 4)), dma((2, 4)), dma((2, 4)), dma((4, 2)),
            dma((MB, NCOL // 2)), dma((MB, NCOL // 2)),
            dma((MB, NCOL // 2)), dma((MB, NCOL // 2)),
            dma((2 * MB,)), dma((2 * MB,)), dma((MB,)), dma((MB,)), dma((2,)), dma((2,)),
            dma((2, NBATCH, 2, 8)), dma((2, NBATCH, 16)),
        ],
        compiler_params=pltpu.CompilerParams(
            collective_id=0, has_side_effects=True, vmem_limit_bytes=56 * 1024 * 1024
        ),
    )(sample_ids, received_before[0], sent_before[0], tokens, cotangent, norm_gain, down_proj[0], up_proj[0])
    return ((grad_down * gain)[None], grad_up[None])


def solution(mesh):
    placed = (
        P(None, "dp", None),
        P(None, "dp", None),
        P("dp", None),
        P("section", "dp", None, None),
        P("section", "dp", None, None),
        P("section", None),
        P("section", "dp", None),
        P("section", None, "dp"),
    )
    return jax.shard_map(
        shards,
        mesh=mesh,
        in_specs=placed,
        out_specs=(P("section", "dp", None), P("section", None, "dp")),
        check_vma=False,
    )
```

```python
import functools

import jax
import jax.numpy as jnp
from jax import lax
from jax.experimental import pallas as pl
from jax.experimental.pallas import tpu as pltpu
from jax.sharding import PartitionSpec as P

MESH = pl.DeviceIdType.MESH
F32, BF16 = jnp.float32, jnp.bfloat16
EPS = 1e-05
D = 8192
HALF = 4096
RANK = 256
TOK = 16
MB = 8
CH = 512
COLS = 512
NCOL = HALF // COLS
STAGES = 8
BATCH = 2 * TOK
NBATCH = MB * TOK // BATCH
PACK = CH + RANK
LOW = 128


def tn(a, b):
    return lax.dot_general(a, b, (((0,), (0,)), ((), ())), preferred_element_type=F32)


def nn(a, b):
    return jnp.dot(a, b, preferred_element_type=F32)


def lanes(v):
    total = v[:, 0:128]
    for k in range(128, v.shape[1], 128):
        total = total + v[:, k : k + 128]
    return total


def kernel(
    ids, rec_in, sent_in, tok_in, cot_in, gain_in, down_in, up_in, gd_out, gu_out,
    raw, perm, gn, rec, sent, wd, wu, wdt, wut, xin, xz, uz, xf, fout, bout, red_tx, red_rx,
    bred_tx, bred_rx, gt_tx, gt_rx, zed_tx, zed_rx, gt, zed, pre, scl, gxz, guz,
    c_raw, s_tok, s_gn, r_gn, s_tab, r_tab, s_w, r_w, s_x, r_x, s_xr, r_xr,
    s_u, r_u, s_v, r_v, s_vr, r_vr,
    s_hf, r_hf, s_hb, r_hb, s_red, r_red, s_br, r_br, s_one, r_one, s_g, r_g,
):
    s = lax.axis_index("section")
    e = lax.axis_index("dp")
    h, z = lax.rem(s, 2), lax.div(s, 2)
    c, q = lax.rem(e, 2), lax.div(e, 2)
    chip = h * 8 + q
    owner_core = lax.div(e, 8)
    local = c == owner_core
    other = (s, e + 1 - 2 * c)

    raw_tok = pltpu.make_async_copy(tok_in, raw, c_raw)
    raw_cot = pltpu.make_async_copy(cot_in, raw, c_raw)

    @pl.when(z == 0)
    def _():
        raw_tok.start()

    @pl.when(z == STAGES - 1)
    def _():
        raw_cot.start()

    barrier = pltpu.get_barrier_semaphore()

    def greet(t, carry):
        place = lax.rem(h * 16 + e + t, 32)
        pl.semaphore_signal(
            barrier, inc=1, device_id=(2 * z + lax.div(place, 16), lax.rem(place, 16)), device_id_type=MESH
        )
        return carry

    lax.fori_loop(1, 32, greet, 0)

    @pl.when(z > 0)
    def _():
        pl.semaphore_signal(barrier, inc=1, device_id=(s - 2, e), device_id_type=MESH)

    @pl.when(z < STAGES - 1)
    def _():
        pl.semaphore_signal(barrier, inc=1, device_id=(s + 2, e), device_id_type=MESH)

    neighbours = jnp.where(z > 0, 1, 0) + jnp.where(z < STAGES - 1, 1, 0)
    pl.semaphore_wait(barrier, 31 + neighbours)

    def table_copy(which, k, t):
        src = (rec_in, sent_in)[which]
        dst = (rec, sent)[which]
        h2, c2 = lax.rem(h + t // 2, 2), lax.rem(c + t, 2)
        row = pl.multiple_of((2 * k + c) * TOK, TOK)
        return dict(
            src_ref=src.at[4 * h2 + k, :, pl.ds(pl.multiple_of(c2 * HALF, HALF), HALF)],
            dst_ref=dst.at[h, pl.ds(row, TOK), :],
        ), s_tab.at[which, k, t], r_tab.at[which, h, 2 * k + c], (2 * z + h2, 2 * q + c2)

    def table_used(which):
        return s != (0, 2 * STAGES - 1)[which]

    def table_start(which, k):
        @pl.when(table_used(which))
        def _():
            for t in range(4):
                refs, ssem, rsem, dev = table_copy(which, k, t)
                if t == 0:
                    pltpu.make_async_copy(refs["src_ref"], refs["dst_ref"], rsem).start()
                else:
                    pltpu.make_async_remote_copy(
                        **refs, send_sem=ssem, recv_sem=rsem, device_id=dev, device_id_type=MESH
                    ).start()

    def table_sent(which, k):
        @pl.when(table_used(which))
        def _():
            for t in range(1, 4):
                refs, ssem, rsem, dev = table_copy(which, k, t)
                pltpu.make_async_remote_copy(
                    **refs, send_sem=ssem, recv_sem=rsem, device_id=dev, device_id_type=MESH
                ).wait_send()

    def end_copies(which, k):
        dst, part = ((rec, 0), (sent, 1))[which]
        place = dst.at[part, pl.ds(pl.multiple_of((2 * k + c) * TOK, TOK), TOK), :]
        rsem = r_tab.at[which, part, 2 * k + c]
        mine = perm.at[k, :, pl.ds(pl.multiple_of(c * HALF, HALF), HALF)]
        return mine, place, rsem

    def end_far(which, k):
        theirs = perm.at[k, :, pl.ds(pl.multiple_of((1 - c) * HALF, HALF), HALF)]
        place, rsem = end_copies(which, k)[1:]
        return pltpu.make_async_remote_copy(
            src_ref=theirs, dst_ref=place, send_sem=s_tok.at[k], recv_sem=rsem, device_id=other, device_id_type=MESH
        )

    def end_start(which):
        (raw_tok, raw_cot)[which].wait()
        for k in range(4):
            at = jnp.int32(0)
            for m in range(1, MB):
                at = jnp.where(ids[0, m] == 4 * h + k, m, at)
            at = jnp.clip(at, 0, MB - 1)

            def move(n, carry, at=at, k=k):
                cols = pl.ds(pl.multiple_of(n * 1024, 1024), 1024)
                perm[k, :, cols] = raw[at, :, cols]
                return carry

            lax.fori_loop(0, D // 1024, move, 0)
            end_far(which, k).start()
            pltpu.make_async_copy(*end_copies(which, k)).start()

    def end_sent(which):
        for k in range(4):
            end_far(which, k).wait_send()

    def table_wait(which, part, i):
        place = (rec, sent)[which].at[part, pl.ds(pl.multiple_of(i * TOK, TOK), TOK), :]
        pltpu.make_async_copy(place, place, r_tab.at[which, part, i]).wait()

    slot = lax.rem(e, 8)
    spot = pl.ds(pl.multiple_of(slot * CH, CH), CH)
    col_x = lax.rem(q, 4)
    row_y = 2 * h + owner_core

    def device(x, y, core):
        return (2 * z + lax.div(y, 2), 8 * lax.rem(y, 2) + 2 * x + core)

    def wide(x):
        return pl.ds(pl.multiple_of(x * 2 * CH, 2 * CH), 2 * CH)

    def away(t):
        return lax.rem(col_x + t, 4)

    def shard(kind, part, j):
        at = pl.ds(pl.multiple_of(j * CH, CH), CH)
        return wd.at[part, at, :] if kind == 0 else wu.at[part, pl.ds(LOW, RANK - LOW), at]

    def w_remote(kind, t):
        return pltpu.make_async_remote_copy(
            src_ref=(down_in, up_in.at[pl.ds(LOW, RANK - LOW), :])[kind], dst_ref=shard(kind, h, slot),
            send_sem=s_w.at[kind, t], recv_sem=r_w.at[kind, h, c],
            device_id=device(col_x, lax.rem(row_y + t, 4), owner_core), device_id_type=MESH,
        )

    def w_first(kind):
        @pl.when(local)
        def _():
            src = (down_in, up_in.at[pl.ds(LOW, RANK - LOW), :])[kind]
            pltpu.make_async_copy(src, shard(kind, h, slot), r_w.at[kind, h, c]).start()

        @pl.when(jnp.logical_not(local))
        def _():
            w_remote(kind, 0).start()

        for t in (1, 3, 2):
            w_remote(kind, t).start()

    def u_remote(t):
        return pltpu.make_async_remote_copy(
            src_ref=up_in.at[pl.ds(0, LOW), :], dst_ref=wu.at[h, pl.ds(0, LOW), spot],
            send_sem=s_u.at[t], recv_sem=r_u.at[slot],
            device_id=device(away(t), row_y, owner_core), device_id_type=MESH,
        )

    def u_first():
        @pl.when(local)
        def _():
            pltpu.make_async_copy(
                up_in.at[pl.ds(0, LOW), :], wu.at[h, pl.ds(0, LOW), spot], r_u.at[slot]
            ).start()

        @pl.when(jnp.logical_not(local))
        def _():
            u_remote(0).start()

        for t in (1, 3, 2):
            u_remote(t).start()

    def first_start():
        w_first(0)
        u_first()
        w_first(1)

    def first_sent():
        @pl.when(jnp.logical_not(local))
        def _():
            w_remote(0, 0).wait_send()
            w_remote(1, 0).wait_send()
            u_remote(0).wait_send()

        for t in range(1, 4):
            w_remote(0, t).wait_send()
            w_remote(1, t).wait_send()
            u_remote(t).wait_send()

    def w_place(kind, part, x):
        return wd.at[part, wide(x), :] if kind == 0 else wu.at[part, pl.ds(LOW, RANK - LOW), wide(x)]

    def w_block(kind, part, t):
        place = w_place(kind, part, col_x)
        return pltpu.make_async_remote_copy(
            src_ref=place, dst_ref=place, send_sem=s_x.at[kind, part, t], recv_sem=r_x.at[kind, part, col_x],
            device_id=(s, e - 2 * col_x + 2 * away(t)), device_id_type=MESH,
        )

    def w_start(kind, part):
        for j in range(2):
            place = shard(kind, part, 2 * col_x + j)
            pltpu.make_async_copy(place, place, r_w.at[kind, part, j]).wait()
        for t in (1, 3):
            w_block(kind, part, t).start()

    def w_half(kind, part, x, half):
        if kind == 0:
            return wd.at[part, pl.ds(pl.multiple_of((2 * x + half) * CH, CH), CH), :]
        return wu.at[part, pl.ds(LOW + half * ((RANK - LOW) // 2), (RANK - LOW) // 2), wide(x)]

    def w_relay(kind, part, half):
        place = w_half(kind, part, away((3, 1)[half]), half)
        return pltpu.make_async_remote_copy(
            src_ref=place, dst_ref=place, send_sem=s_xr.at[kind, part, half], recv_sem=r_xr.at[kind, part, half],
            device_id=(s, e - 2 * col_x + 2 * away((1, 3)[half])), device_id_type=MESH,
        )

    def w_forward(kind, part):
        for half in range(2):
            x = away((3, 1)[half])
            place = w_place(kind, part, x)
            pltpu.make_async_copy(place, place, r_x.at[kind, part, x]).wait()
            w_relay(kind, part, half).start()

    def u_block(n, t):
        place = wu.at[h, pl.ds(0, LOW), wide(away(n))]
        return pltpu.make_async_remote_copy(
            src_ref=place, dst_ref=place, send_sem=s_v.at[n, t], recv_sem=r_v.at[h, away(n)],
            device_id=device(col_x, lax.rem(row_y + t, 4), c), device_id_type=MESH,
        )

    def u_start(n):
        @pl.when(local)
        def _():
            for j in range(2):
                at = 2 * away(n) + j
                place = wu.at[h, pl.ds(0, LOW), pl.ds(pl.multiple_of(at * CH, CH), CH)]
                pltpu.make_async_copy(place, place, r_u.at[at]).wait()
            for t in (1, 3):
                u_block(n, t).start()

    y_me = 2 * h + lax.div(e, 8)

    def u_half(part, n, half):
        return wu.at[part, pl.ds(pl.multiple_of(half * (LOW // 2), LOW // 2), LOW // 2), wide(away(n))]

    def u_relay(part, n):
        half = jnp.where(lax.rem(y_me - 2 * part - c + 4, 4) == 1, 0, 1)
        place = u_half(part, n, half)
        return pltpu.make_async_remote_copy(
            src_ref=place, dst_ref=place, send_sem=s_vr.at[part, n], recv_sem=r_vr.at[n, half],
            device_id=device(col_x, lax.rem(y_me + 1 + 2 * half, 4), c), device_id_type=MESH,
        )

    def u_forward(n):
        @pl.when(jnp.logical_not(local))
        def _():
            for part in range(2):
                place = wu.at[part, pl.ds(0, LOW), wide(away(n))]
                pltpu.make_async_copy(place, place, r_v.at[part, away(n)]).wait()
                u_relay(part, n).start()

    def weight_wait(kind, part):
        for half in range(2):
            place = w_half(kind, part, away(2), half)
            pltpu.make_async_copy(place, place, r_xr.at[kind, part, half]).wait()
        if kind == 1:
            @pl.when(jnp.logical_and(local, h != part))
            def _():
                for n in range(4):
                    for half in range(2):
                        place = u_half(part, n, half)
                        pltpu.make_async_copy(place, place, r_vr.at[n, half]).wait()

    def weight_sent():
        first_sent()
        for kind in range(2):
            for part in range(2):
                for t in (1, 3):
                    w_block(kind, part, t).wait_send()
                for half in range(2):
                    w_relay(kind, part, half).wait_send()

        @pl.when(local)
        def _():
            for n in range(4):
                for t in (1, 3):
                    u_block(n, t).wait_send()

        @pl.when(jnp.logical_not(local))
        def _():
            for n in range(4):
                for part in range(2):
                    u_relay(part, n).wait_send()

    gain_part = gain_in.at[:, pl.ds(pl.multiple_of(c * HALF, HALF), HALF)]
    gain_near = pltpu.make_async_copy(gain_part, gn.at[h], r_gn.at[h])
    gain_far = pltpu.make_async_remote_copy(
        src_ref=gain_part, dst_ref=gn.at[h], send_sem=s_gn, recv_sem=r_gn.at[h],
        device_id=(s + 1 - 2 * h, e), device_id_type=MESH,
    )

    first_start()
    gain_near.start()
    gain_far.start()
    table_start(0, 0)
    table_start(1, 0)

    @pl.when(z == 0)
    def _():
        end_start(0)

    @pl.when(z == STAGES - 1)
    def _():
        end_start(1)

    w_start(0, h)
    u_start(0)
    w_start(1, h)
    w_start(0, 1 - h)
    w_start(1, 1 - h)
    for n in (1, 3, 2):
        u_start(n)
    w_forward(0, h)
    u_forward(0)
    w_forward(1, h)
    u_forward(1)
    table_start(0, 1)
    table_start(1, 1)
    u_forward(3)
    w_forward(0, 1 - h)
    u_forward(2)
    w_forward(1, 1 - h)
    for part in range(2):
        pltpu.make_async_copy(gn.at[part], gn.at[part], r_gn.at[part]).wait()

    def red_copy(n):
        return pltpu.make_async_remote_copy(
            src_ref=red_tx.at[n], dst_ref=red_rx.at[n], send_sem=s_red.at[n], recv_sem=r_red.at[n],
            device_id=other, device_id_type=MESH,
        )

    def bred_copy(i):
        return pltpu.make_async_remote_copy(
            src_ref=bred_tx.at[i], dst_ref=bred_rx.at[i], send_sem=s_br.at[i], recv_sem=r_br.at[i],
            device_id=other, device_id_type=MESH,
        )

    def one_copy(n):
        src, dst = ((gt_tx, gt_rx), (zed_tx, zed_rx))[n]
        return pltpu.make_async_remote_copy(
            src_ref=src, dst_ref=dst, send_sem=s_one.at[n], recv_sem=r_one.at[n], device_id=other, device_id_type=MESH
        )

    def col(n):
        return slice(n * COLS, (n + 1) * COLS)

    def hop(n, i, ahead):
        rows = pl.ds(pl.multiple_of(i * TOK, TOK), TOK)
        if ahead:
            wide_col = slice(2 * n * COLS, 2 * (n + 1) * COLS)
            src, dst, ss, rs, dev = fout.at[rows, wide_col], xin.at[rows, wide_col], s_hf, r_hf, (s + 2, e)
        else:
            two = pl.ds(2 * n, 2)
            src, dst, ss, rs, dev = bout.at[two, rows, :], uz.at[1, two, rows, pl.ds(0, CH)], s_hb, r_hb, (s - 2, e)
        return pltpu.make_async_remote_copy(
            src_ref=src, dst_ref=dst, send_sem=ss.at[i, n], recv_sem=rs.at[i, n], device_id=dev, device_id_type=MESH
        )

    def rows_copy(kind, b, part, j):
        src = (xz, uz)[kind].at[part, j, pl.ds(pl.multiple_of(b * BATCH, BATCH), BATCH), :]
        return src, landing(kind, b, chip), s_g.at[kind, b, part, j], r_g.at[kind, b, chip], (2 * z + part, 8 * c + j)

    def landing(kind, b, source):
        at = pl.ds(pl.multiple_of((16 * b + source) * BATCH, BATCH), BATCH)
        return (gxz, guz)[kind].at[at, :]

    def rows_each(kind, b, own, far):
        def one(t, carry):
            place = lax.rem(chip + t, 16)
            part, j = lax.div(place, 8), lax.rem(place, 8)
            src, dst, ssem, rsem, dev = rows_copy(kind, b, part, j)
            mine = jnp.logical_and(h == part, 8 * c + j == e)
            if own:
                @pl.when(mine)
                def _():
                    pltpu.make_async_copy(src, dst, rsem).start()

            @pl.when(jnp.logical_not(mine))
            def _():
                far(
                    pltpu.make_async_remote_copy(
                        src_ref=src, dst_ref=dst, send_sem=ssem, recv_sem=rsem, device_id=dev, device_id_type=MESH
                    )
                )

            return carry

        lax.fori_loop(0, 16, one, 0, unroll=4)

    def rows_start(kind, b):
        rows_each(kind, b, True, lambda copy: copy.start())

    def rows_sent(kind, b):
        rows_each(kind, b, False, lambda copy: copy.wait_send())

    def rows_wait(kind, b):
        def one(t, carry):
            place = landing(kind, b, t)
            pltpu.make_async_copy(place, place, r_g.at[kind, b, t]).wait()
            return carry

        lax.fori_loop(0, 16, one, 0)

    def turn():
        for part in range(2):
            def one(j, carry, part=part):
                at = pl.ds(pl.multiple_of(j * CH, CH), CH)
                wdt[part, :, at] = wd[part, at, :].T
                wut[part, at, :] = wu[part, :, at].T
                return carry

            lax.fori_loop(0, HALF // CH, one, 0)

        gt_tx[...] = jnp.zeros_like(gt_tx)

        def product(j, carry):
            at = pl.ds(pl.multiple_of(j * CH, CH), CH)
            gt_tx[...] += nn((wdt[1, :, at].astype(F32) * gn[1, :, at]).astype(BF16), wut[0, at, :])
            return carry

        lax.fori_loop(0, HALF // CH, product, 0)
        one_copy(0).start()
        one_copy(0).wait_recv()
        gt[...] = (gt_tx[...] + gt_rx[...]).astype(BF16)

    late = z >= STAGES // 2

    @pl.when(late)
    def _():
        for kind in range(2):
            for part in range(2):
                weight_wait(kind, part)
        turn()

    def forward(i, carry):
        rows = pl.ds(pl.multiple_of(i * TOK, TOK), TOK)
        fresh = jnp.logical_and(i == 0, jnp.logical_not(late))
        table_wait(0, 0, i)

        @pl.when(i == 0)
        def _():
            table_start(0, 2)
            table_start(1, 2)

        @pl.when(i == 2)
        def _():
            table_start(0, 3)
            table_start(1, 3)


        @pl.when(fresh)
        def _():
            weight_wait(0, 0)

        acc = jnp.zeros((TOK, RANK), F32)
        sq = jnp.zeros((TOK, 128), F32)
        for n in range(NCOL):
            @pl.when(z > 0)
            def _():
                if n % 2 == 0:
                    hop(n // 2, i, True).wait_recv()
                xf[:, col(n)] = rec[0, rows, col(n)].astype(F32) + xin[rows, col(n)].astype(F32)

            @pl.when(z == 0)
            def _():
                xf[:, col(n)] = rec[0, rows, col(n)].astype(F32)

            x = xf[:, col(n)]
            xz[0, n, rows, 0:CH] = x.astype(BF16)
            sq = sq + lanes(x * x)
            acc = acc + nn((x * gn[0, :, col(n)]).astype(BF16), wd[0, col(n), :])

        def finish(part, acc, sq):
            n = 2 * i + part
            red_tx[n, :, 0:RANK] = acc
            red_tx[n, :, RANK:] = sq
            red_copy(n).start()
            red_copy(n).wait_recv()
            total = acc + red_rx[n, :, 0:RANK]
            square = jnp.sum(sq + red_rx[n, :, RANK:], axis=1, keepdims=True)
            scale = lax.rsqrt(square * (1.0 / D) + EPS)
            v = total * scale
            pre[part, rows, :] = v
            scl[part, rows, :] = jnp.broadcast_to(scale, (TOK, 128))
            a = (v * jax.nn.sigmoid(v)).astype(BF16)
            for j in range(8):
                xz[part, j, rows, CH:] = a
            return a

        a = finish(0, acc, sq)

        @pl.when(fresh)
        def _():
            weight_wait(1, 0)
            weight_wait(0, 1)

        table_wait(0, 1, i)
        table_wait(1, 0, i)
        acc = jnp.zeros((TOK, RANK), F32)
        sq = jnp.zeros((TOK, 128), F32)
        for n in range(NCOL):
            x = (
                xf[:, col(n)] + nn(a, wu[0, :, col(n)])
                + (rec[1, rows, col(n)].astype(F32) - sent[0, rows, col(n)].astype(F32))
            )
            xf[:, col(n)] = x
            xz[1, n, rows, 0:CH] = x.astype(BF16)
            sq = sq + lanes(x * x)
            acc = acc + nn((x * gn[1, :, col(n)]).astype(BF16), wd[1, col(n), :])
        a = finish(1, acc, sq)

        @pl.when(fresh)
        def _():
            weight_wait(1, 1)

        table_wait(1, 1, i)

        @pl.when(z < STAGES - 1)
        def _():
            for n in range(NCOL):
                x = xf[:, col(n)] + nn(a, wu[1, :, col(n)]) - sent[1, rows, col(n)].astype(F32)
                fout[rows, col(n)] = x.astype(BF16)
                if n % 2 == 1:
                    hop(n // 2, i, True).start()

        return carry

    lax.fori_loop(0, MB, forward, 0)

    @pl.when(jnp.logical_not(late))
    def _():
        turn()

    zed_tx[...] = jnp.zeros_like(zed_tx)
    for n in range(NCOL):
        zed_tx[...] += nn(xz[1, n, :, 0:CH], wut[0, col(n), :])
    one_copy(1).start()

    def early():
        def one(b, carry):
            rows_start(0, b)
            return carry

        lax.fori_loop(0, NBATCH, one, 0)

    @pl.when(z < STAGES - 1)
    def _():
        early()

    def backward(i, carry):
        rows = pl.ds(pl.multiple_of(i * TOK, TOK), TOK)

        def slope(part):
            v = pre[part, rows, :]
            gate = jax.nn.sigmoid(v)
            return v, gate * (1.0 + v * (1.0 - gate)), scl[part, rows, 0:1]

        v1, slope1, scale1 = slope(1)
        v0, slope0, scale0 = slope(0)
        acc1 = jnp.zeros((TOK, RANK), F32)
        acc0 = jnp.zeros((TOK, RANK), F32)
        for n in range(NCOL):
            if n % 2 == 0:
                @pl.when(z < STAGES - 1)
                def _():
                    hop(n // 2, i, False).wait_recv()

            @pl.when(z == STAGES - 1)
            def _():
                uz[1, n, rows, 0:CH] = sent[1, rows, col(n)]

            u = uz[1, n, rows, 0:CH]
            acc1 = acc1 + nn(u, wut[1, col(n), :])
            acc0 = acc0 + nn(u, wut[0, col(n), :])
        bred_tx[i, :, 0:RANK] = acc1
        bred_tx[i, :, RANK:] = acc0
        bred_copy(i).start()

        @pl.when(i == 0)
        def _():
            one_copy(1).wait_recv()
            zed[...] = zed_tx[...] + zed_rx[...]

        bred_copy(i).wait_recv()

        def finish(d_pre, v, scale):
            mean = jnp.sum(d_pre * v, axis=1, keepdims=True) * (1.0 / D)
            return (d_pre * scale).astype(BF16), mean * scale * scale

        back1, shrink1 = finish((acc1 + bred_rx[i, :, 0:RANK]) * slope1, v1, scale1)
        d_act = acc0 + bred_rx[i, :, RANK:] + nn(back1, gt[...]) - shrink1 * zed[rows, :]
        back0, shrink0 = finish(d_act * slope0, v0, scale0)
        for n in range(NCOL):
            u = (
                uz[1, n, rows, 0:CH].astype(F32) + nn(back1, wdt[1, :, col(n)]) * gn[1, :, col(n)]
                - shrink1 * xz[1, n, rows, 0:CH].astype(F32)
            ).astype(BF16)
            uz[0, n, rows, 0:CH] = u
            u = (
                u.astype(F32) + nn(back0, wdt[0, :, col(n)]) * gn[0, :, col(n)]
                - shrink0 * xz[0, n, rows, 0:CH].astype(F32)
            )
            bout[n, rows, :] = u.astype(BF16)
            if n % 2 == 1:
                @pl.when(z > 0)
                def _():
                    hop(n // 2, i, False).start()

        for n in range(NCOL):
            uz[1, n, rows, CH:] = back1
            uz[0, n, rows, CH:] = back0
        return carry

    def back_batch(b, carry):
        lax.fori_loop(b * (BATCH // TOK), (b + 1) * (BATCH // TOK), backward, 0)
        rows_start(1, b)
        return carry

    lax.fori_loop(0, NBATCH, back_batch, 0)

    @pl.when(z == STAGES - 1)
    def _():
        early()

    weight_sent()
    gain_far.wait_send()

    @pl.when(z == 0)
    def _():
        end_sent(0)

    @pl.when(z == STAGES - 1)
    def _():
        end_sent(1)

    for k in range(4):
        table_sent(0, k)
        table_sent(1, k)

    def rest(i, carry):
        for n in range(NCOL // 2):
            @pl.when(z < STAGES - 1)
            def _():
                hop(n, i, True).wait_send()

            @pl.when(z > 0)
            def _():
                hop(n, i, False).wait_send()

        for k in range(2):
            red_copy(2 * i + k).wait_send()
        bred_copy(i).wait_send()
        return carry

    lax.fori_loop(0, MB, rest, 0)
    one_copy(0).wait_send()
    one_copy(1).wait_send()

    def rows_gone(b, carry):
        rows_sent(0, b)

        @pl.when(b < NBATCH - 1)
        def _():
            rows_sent(1, b)

        return carry

    lax.fori_loop(0, NBATCH, rows_gone, 0)

    gd_out[...] = jnp.zeros_like(gd_out)
    gu_out[...] = jnp.zeros_like(gu_out)

    def total(b, carry):
        rows_wait(0, b)
        rows_wait(1, b)
        at = pl.ds(pl.multiple_of(16 * BATCH * b, 16 * BATCH), 16 * BATCH)
        gd_out[...] += tn(gxz[at, 0:CH], guz[at, CH:])
        gu_out[...] += tn(gxz[at, CH:], guz[at, 0:CH])
        return carry

    lax.fori_loop(0, NBATCH, total, 0)
    rows_sent(1, NBATCH - 1)


def shards(tokens, cotangent, sample_ids, sent_before, received_before, norm_gain, down_proj, up_proj):
    e = lax.axis_index("dp")
    gain = lax.dynamic_slice(norm_gain[0], (e * CH,), (CH,))[:, None]
    any_ = pl.BlockSpec(memory_space=pl.ANY)
    vmem = pl.BlockSpec(memory_space=pltpu.VMEM)
    dma = pltpu.SemaphoreType.DMA
    rows = MB * TOK
    grad_down, grad_up = pl.pallas_call(
        kernel,
        out_shape=(jax.ShapeDtypeStruct((CH, RANK), F32), jax.ShapeDtypeStruct((RANK, CH), F32)),
        in_specs=[pl.BlockSpec(memory_space=pltpu.SMEM)] + [any_] * 7,
        out_specs=(vmem, vmem),
        scratch_shapes=[
            pltpu.VMEM((MB, TOK, D), BF16),
            pltpu.VMEM((4, TOK, D), BF16),
            pltpu.VMEM((2, 1, HALF), F32),
            pltpu.VMEM((2, rows, HALF), BF16),
            pltpu.VMEM((2, rows, HALF), BF16),
            pltpu.VMEM((2, HALF, RANK), BF16),
            pltpu.VMEM((2, RANK, HALF), BF16),
            pltpu.VMEM((2, RANK, HALF), BF16),
            pltpu.VMEM((2, HALF, RANK), BF16),
            pltpu.VMEM((rows, HALF), BF16),
            pltpu.VMEM((2, 8, rows, PACK), BF16),
            pltpu.VMEM((2, 8, rows, PACK), BF16),
            pltpu.VMEM((TOK, HALF), F32),
            pltpu.VMEM((rows, HALF), BF16),
            pltpu.VMEM((8, rows, CH), BF16),
            pltpu.VMEM((2 * MB, TOK, RANK + 128), F32),
            pltpu.VMEM((2 * MB, TOK, RANK + 128), F32),
            pltpu.VMEM((MB, TOK, 2 * RANK), F32),
            pltpu.VMEM((MB, TOK, 2 * RANK), F32),
            pltpu.VMEM((RANK, RANK), F32),
            pltpu.VMEM((RANK, RANK), F32),
            pltpu.VMEM((rows, RANK), F32),
            pltpu.VMEM((rows, RANK), F32),
            pltpu.VMEM((RANK, RANK), BF16),
            pltpu.VMEM((rows, RANK), F32),
            pltpu.VMEM((2, rows, RANK), F32),
            pltpu.VMEM((2, rows, 128), F32),
            pltpu.VMEM((16 * rows, PACK), BF16),
            pltpu.VMEM((16 * rows, PACK), BF16),
            dma, dma((4,)),
            dma, dma((2,)),
            dma((2, 4, 4)), dma((2, 2, MB)),
            dma((2, 4)), dma((2, 2, 2)), dma((2, 2, 4)), dma((2, 2, 4)), dma((2, 2, 2)), dma((2, 2, 2)),
            dma((4,)), dma((8,)), dma((4, 4)), dma((2, 4)), dma((2, 4)), dma((4, 2)),
            dma((MB, NCOL // 2)), dma((MB, NCOL // 2)),
            dma((MB, NCOL // 2)), dma((MB, NCOL // 2)),
            dma((2 * MB,)), dma((2 * MB,)), dma((MB,)), dma((MB,)), dma((2,)), dma((2,)),
            dma((2, NBATCH, 2, 8)), dma((2, NBATCH, 16)),
        ],
        compiler_params=pltpu.CompilerParams(
            collective_id=0, has_side_effects=True, vmem_limit_bytes=56 * 1024 * 1024
        ),
    )(sample_ids, received_before[0], sent_before[0], tokens, cotangent, norm_gain, down_proj[0], up_proj[0])
    return ((grad_down * gain)[None], grad_up[None])


def solution(mesh):
    placed = (
        P(None, "dp", None),
        P(None, "dp", None),
        P("dp", None),
        P("section", "dp", None, None),
        P("section", "dp", None, None),
        P("section", None),
        P("section", "dp", None),
        P("section", None, "dp"),
    )
    return jax.shard_map(
        shards,
        mesh=mesh,
        in_specs=placed,
        out_specs=(P("section", "dp", None), P("section", None, "dp")),
        check_vma=False,
    )
```
